256 devices in a mesh: expert: 32 (over y, x, core), dp: 8 (over z).
Axes of the slice: x: 4, y: 4, z: 8, core: 2. Of those that a mesh axis runs over, the one named last changes fastest.
Arguments:
- tokens: bfloat16 [12288, 2048], P(('expert', 'dp')), may hold values from -6 to 6
- routes: int32 [12288, 8], P(('expert', 'dp')), may hold values from 0 to 31, all different within a row; in each aligned block of 48 rows (0 to 47, 48 to 95, ...) at most 16 rows name the same one
- gate_weights: float32 [12288, 8], P(('expert', 'dp')), may hold values from 0.05 to 0.3
- w_gate: bfloat16 [32, 2048, 768], P('expert'), may hold values from -0.125 to 0.125
- w_up: bfloat16 [32, 2048, 768], P('expert'), may hold values from -0.125 to 0.125
- w_down: bfloat16 [32, 768, 2048], P('expert'), may hold values from -0.21875 to 0.21875
- out_grad: bfloat16 [12288, 2048], P(('expert', 'dp')), may hold values from -6 to 6
Outputs:
- layer_out: bfloat16 [12288, 2048], P(('expert', 'dp'))
- token_grad: bfloat16 [12288, 2048], P(('expert', 'dp'))
- gate_weights_grad: float32 [12288, 8], P(('expert', 'dp'))
- w_gate_grad: float32 [32, 2048, 768], P('expert', 'dp')
- w_up_grad: float32 [32, 2048, 768], P('expert', 'dp')
- w_down_grad: float32 [32, 768, 2048], P('expert', None, 'dp')
The draws below stay inside these ranges and needn't reach their ends.
Inputs may be any that keep to these rules, and one draw needn't show every extreme that they name: `routes`: each token names 8 different experts; within the rows of one device (aligned blocks of 48 rows) no expert is named more than 16 times, a bound that some block reaches.
All inputs are finite; a program needn't handle non-finite values.
Results may differ from the reference program's by a relative error of at most 0.015.
Values may be sent and summed in bfloat16 or wider, within the bound.
No kernel may reach another device: no remote copies, remote signals or barrier semaphores. Data moves between devices by JAX's collectives and lax.ppermute only.
A program may use at most 128 MiB of HBM per device.

```python
import math
import jax
import jax.numpy as jnp
import numpy as np
from jax import lax

D = 2048
FF = 768
TOP = 8
TOK_DEV = 48
EXPERTS = 32
CAP = 16
TOKENS = 12288
N_EXPERT = 32
N_DP = 8


def shard_levels(stream_key, shape, shards, least, largest):
    def one(dim, blocks):
        draws = jax.random.uniform(jax.random.fold_in(jax.random.fold_in(stream_key, 6), dim), (blocks,), jnp.float32, least / len(shards), largest / len(shards))
        return jnp.repeat(jnp.exp(draws), shape[dim] // blocks).reshape((-1,) + (1,) * (len(shape) - dim - 1))

    level = one(*shards[0])
    for cut in shards[1:]:
        level = level * one(*cut)
    return level


def assign_block(stream_key, own, number, rows, number_of, top, bound, lean):
    order = jax.random.permutation(stream_key, number_of)
    heavy_load, common = portions_of(number_of, rows * top, bound, lean, True), portions_of(number_of, rows * top, bound, lean, False)
    places = jnp.arange(number_of)

    def named(tallies, offset_by):
        used = int((tallies > 0).sum())
        fixed = max(1, used // 4)
        moved = fixed + (places - fixed + offset_by * (used - fixed)) % max(1, number_of - fixed)
        return jnp.zeros((number_of,), jnp.int32).at[order[jnp.where(places < fixed, places, moved)]].set(jnp.asarray(tallies, jnp.int32))

    tallies = jnp.where(number % 4 == 0, named(heavy_load, number // 4), named(common, number - number // 4 - 1))
    mixed = jax.random.permutation(jax.random.fold_in(own, 3), number_of)
    giver, sink = mixed[0:number_of // 2 * 2:2], mixed[1:number_of // 2 * 2:2]
    slack = jnp.minimum(tallies[giver] - 1, bound - tallies[sink]) // 2
    slack = jnp.where((giver == order[0]) | (sink == order[0]) | (tallies[sink] == 0), 0, jnp.maximum(slack, 0))
    moved = jax.random.randint(jax.random.fold_in(own, 4), (number_of // 2,), 0, 1 << 20) % (slack + 1)
    tallies = tallies.at[giver].add(-moved).at[sink].add(moved)
    members = jnp.searchsorted(jnp.cumsum(tallies), jnp.arange(rows * top), side="right").astype(jnp.int32)
    table = members.reshape(top, rows).T
    table = table[jax.random.permutation(jax.random.fold_in(own, 1), rows)]
    offset_by = jax.random.randint(jax.random.fold_in(own, 2), (rows, 1), 0, top)
    return jnp.take_along_axis(table, (jnp.arange(top)[None, :] + offset_by) % top, axis=1)


def portions_of(amount, total, reach, lean, full):
    loads = [(1 << 20) // math.isqrt(standing ** lean) + 1 for standing in range(1, amount + 1)]
    largest = reach if full else min(reach, max(-(-total // amount), total * loads[0] // sum(loads)))
    least = 1 if total - largest >= amount - 1 else 0
    given, surplus = [largest] + [least] * (amount - 1), total - largest - least * (amount - 1)
    while surplus > 0:
        candidates = [i for i in range(1, amount) if given[i] < largest] or [i for i in range(1, amount) if given[i] < reach]
        whole, left = sum([loads[i] for i in candidates]), surplus
        for i in candidates:
            extra = min(reach - given[i], max(1, left * loads[i] // whole), surplus)
            given[i] = given[i] + extra
            surplus = surplus - extra
    return np.array(given)


def bell_draw(key, shape, width, bound, split=(), kind=jnp.bfloat16):
    level = shard_levels(key, shape, split, -0.22, 0.18) if split else 1.0
    result = jax.random.normal(key, shape, jnp.float32) * width * level
    return jnp.minimum(jnp.maximum(result, -bound), bound).astype(kind)


def setup_inputs(seed: int = 0) -> dict:
    arg_keys = jax.random.split(jax.random.key(seed), 8)
    tokens = bell_draw(arg_keys[0], (TOKENS, D), 1.0, 6.0, ((0, 256),))
    routes_keys = jax.random.split(jax.random.fold_in(arg_keys[1], 1), TOKENS // TOK_DEV)
    routes_turns = jax.random.permutation(jax.random.fold_in(arg_keys[1], 3), TOKENS // TOK_DEV)
    routes = jax.vmap(lambda own, number: assign_block(jax.random.fold_in(arg_keys[1], 2), own, number, TOK_DEV, EXPERTS, TOP, CAP, 2))(routes_keys, routes_turns).reshape((TOKENS, TOP))
    gate_weights = jnp.clip(0.05 + 0.25 * jax.random.uniform(arg_keys[2], (TOKENS, TOP), jnp.float32) ** shard_levels(arg_keys[2], (TOKENS, TOP), ((0, 256),), -0.2, 0.2), 0.05, 0.3)
    w_gate = bell_draw(arg_keys[3], (EXPERTS, D, FF), D ** -0.5, 0.125, ((0, 32),))
    w_up = bell_draw(arg_keys[4], (EXPERTS, D, FF), D ** -0.5, 0.125, ((0, 32),))
    w_down = bell_draw(arg_keys[5], (EXPERTS, FF, D), FF ** -0.5, 0.21875, ((0, 32),))
    out_grad = bell_draw(arg_keys[6], (TOKENS, D), 1.0, 6.0, ((0, 256),))
    return dict(tokens=tokens, routes=routes, gate_weights=gate_weights, w_gate=w_gate, w_up=w_up, w_down=w_down, out_grad=out_grad)


def expert_forward(row_block, w_gate_e, w_up_e, w_down_e):
    pre_gate = jnp.dot(row_block, w_gate_e, preferred_element_type=jnp.float32)
    pre_up = jnp.dot(row_block, w_up_e, preferred_element_type=jnp.float32)
    hidden = (jax.nn.silu(pre_gate) * pre_up).astype(jnp.bfloat16)
    output = jnp.dot(hidden, w_down_e, preferred_element_type=jnp.float32).astype(jnp.bfloat16)
    return pre_gate, pre_up, hidden, output


def expert_backward(row_block, pre_gate, pre_up, hidden, grad_block, w_gate_e, w_up_e, w_down_e):
    contract_last = (((1,), (1,)), ((), ()))
    contract_first = (((0,), (0,)), ((), ()))
    hidden_grad = lax.dot_general(grad_block, w_down_e, contract_last, preferred_element_type=jnp.float32)
    sigmoid_gate = jax.nn.sigmoid(pre_gate)
    gate_pre_grad = (hidden_grad * pre_up * sigmoid_gate * (1.0 + pre_gate * (1.0 - sigmoid_gate))).astype(jnp.bfloat16)
    up_pre_grad = (hidden_grad * pre_gate * sigmoid_gate).astype(jnp.bfloat16)
    row_grad = lax.dot_general(gate_pre_grad, w_gate_e, contract_last, preferred_element_type=jnp.float32)
    row_grad = row_grad + lax.dot_general(up_pre_grad, w_up_e, contract_last, preferred_element_type=jnp.float32)
    gate_part = lax.dot_general(row_block, gate_pre_grad, contract_first, preferred_element_type=jnp.float32)
    up_part = lax.dot_general(row_block, up_pre_grad, contract_first, preferred_element_type=jnp.float32)
    down_part = lax.dot_general(hidden, grad_block, contract_first, preferred_element_type=jnp.float32)
    return row_grad.astype(jnp.bfloat16), gate_part, up_part, down_part


def rounded(partial_value):
    return lax.optimization_barrier(partial_value.astype(jnp.bfloat16)).astype(jnp.float32)


def reference(tokens, routes, gate_weights, w_gate, w_up, w_down, out_grad):
    assign_count = TOKENS * TOP
    rows_most = N_EXPERT * CAP
    key_count = EXPERTS * N_DP
    flat_expert = routes.reshape(-1).astype(jnp.int32)
    flat_token = (jnp.arange(assign_count, dtype=jnp.int32) // TOP).astype(jnp.int32)
    flat_gate = gate_weights.reshape(-1)
    dp_group = (flat_token // TOK_DEV) % N_DP
    group_key = (flat_expert * N_DP + dp_group).astype(jnp.int32)
    sorted_order = jnp.argsort(group_key, stable=True).astype(jnp.int32)
    counts = jax.ops.segment_sum(jnp.ones((assign_count,), jnp.int32), group_key, num_segments=key_count).astype(jnp.int32)
    starts = (jnp.cumsum(counts) - counts).astype(jnp.int32)
    position = jnp.zeros((assign_count,), jnp.int32).at[sorted_order].set(jnp.arange(assign_count, dtype=jnp.int32))
    offsets = jnp.arange(rows_most, dtype=jnp.int32)

    def one_group(w_gate_e, w_up_e, w_down_e, key_index):
        live_mask = offsets < counts[key_index]
        picked = sorted_order[jnp.clip(starts[key_index] + offsets, 0, assign_count - 1)]
        token_ids = flat_token[picked]
        row_block = jnp.where(live_mask[:, None], tokens[token_ids], jnp.zeros((), tokens.dtype))
        scaled = (flat_gate[picked][:, None] * out_grad[token_ids].astype(jnp.float32)).astype(jnp.bfloat16)
        grad_block = jnp.where(live_mask[:, None], scaled, jnp.zeros((), scaled.dtype))
        pre_gate, pre_up, hidden, output = expert_forward(row_block, w_gate_e, w_up_e, w_down_e)
        row_grad, gate_part, up_part, down_part = expert_backward(row_block, pre_gate, pre_up, hidden, grad_block, w_gate_e, w_up_e, w_down_e)
        return output, row_grad, (gate_part, up_part, down_part)

    def one_expert(operands):
        expert_id, w_gate_e, w_up_e, w_down_e = operands

        def dp_turn(totals, dp_index):
            output, row_grad, grad_parts = one_group(w_gate_e, w_up_e, w_down_e, expert_id * N_DP + dp_index)
            totals = tuple(running + rounded(partial_value) for running, partial_value in zip(totals, grad_parts))
            return totals, (output, row_grad)

        initial = (jnp.zeros((D, FF), jnp.float32), jnp.zeros((D, FF), jnp.float32), jnp.zeros((FF, D), jnp.float32))
        totals, (outputs, row_grads) = lax.scan(dp_turn, initial, jnp.arange(N_DP, dtype=jnp.int32))
        return totals, outputs, row_grads

    grad_totals, outputs, row_grads = lax.map(one_expert, (jnp.arange(EXPERTS, dtype=jnp.int32), w_gate, w_up, w_down))
    flat_index = group_key * rows_most + (position - starts[group_key])
    assign_out = outputs.reshape(-1, D)[flat_index].reshape(TOKENS, TOP, D)
    assign_grad = row_grads.reshape(-1, D)[flat_index].reshape(TOKENS, TOP, D)
    assign_wide = assign_out.astype(jnp.float32)
    layer_out = jnp.einsum("tk,tkd->td", gate_weights.astype(jnp.float32), assign_wide).astype(jnp.bfloat16)
    gate_weights_grad = jnp.einsum("td,tkd->tk", out_grad.astype(jnp.float32), assign_wide)
    token_grad = jnp.sum(assign_grad.astype(jnp.float32), axis=1).astype(jnp.bfloat16)
    return layer_out, token_grad, gate_weights_grad, grad_totals[0], grad_totals[1], grad_totals[2]
```

```python
import functools

import jax
import jax.numpy as jnp
from jax import lax
from jax.experimental import pallas as pl
from jax.experimental.pallas import tpu as pltpu
from jax.sharding import PartitionSpec as P

BF16 = jnp.bfloat16
F32 = jnp.float32
LAST = (((1,), (1,)), ((), ()))
FIRST = (((0,), (0,)), ((), ()))
VMEM_LIMIT = 56 * 2**20


def params():
    return pltpu.CompilerParams(vmem_limit_bytes=VMEM_LIMIT)


def cost(flops, nbytes, exps=0):
    return pl.CostEstimate(flops=flops, bytes_accessed=nbytes, transcendentals=exps)


def dot(a, b, dims=(((1,), (0,)), ((), ()))):
    return lax.dot_general(a, b, dims, preferred_element_type=F32)


def slot_masks(routes_t, slots, capacity):
    tokens = routes_t.shape[1]
    expert = lax.broadcasted_iota(jnp.int32, (slots, tokens), 0) // capacity
    return [expert == routes_t[k : k + 1, :] for k in range(routes_t.shape[0])]


def dispatch_kernel(capacity, routes_ref, gates_ref, tokens_ref, grads_ref, rows_ref, scaled_ref, place_ref):
    routes_t, gates_t = routes_ref[...], gates_ref[...]
    slots, tokens = place_ref.shape
    masks = slot_masks(routes_t, slots, capacity)
    hit = jnp.zeros((slots, tokens), F32)
    weight = jnp.zeros((slots, tokens), F32)
    for k, mask in enumerate(masks):
        hit = jnp.where(mask, 1.0, hit)
        weight = jnp.where(mask, gates_t[k : k + 1, :], weight)
    before = (
        lax.broadcasted_iota(jnp.int32, (tokens, tokens), 0)
        < lax.broadcasted_iota(jnp.int32, (tokens, tokens), 1)
    ).astype(F32).astype(BF16)
    rank = dot(hit.astype(BF16), before)
    mine = (lax.broadcasted_iota(jnp.int32, (slots, tokens), 0) % capacity).astype(F32)
    place = jnp.where(rank == mine, hit, 0.0)
    slot_weight = jnp.sum(place * weight, axis=1, keepdims=True)
    place_low = place.astype(BF16)
    place_ref[...] = place_low
    rows_ref[...] = dot(place_low, tokens_ref[...]).astype(BF16)
    scaled_ref[...] = (slot_weight * dot(place_low, grads_ref[...])).astype(BF16)


def forward_kernel(rows_ref, gate_ref, up_ref, hidden_ref, gate_slope_ref, up_slope_ref):
    rows = rows_ref[...]
    pre_gate = dot(rows, gate_ref[...])
    pre_up = dot(rows, up_ref[...])
    sig = jax.nn.sigmoid(pre_gate)
    silu = pre_gate * sig
    hidden_ref[...] = (silu * pre_up).astype(BF16)
    gate_slope_ref[...] = pre_up * sig * (1.0 + pre_gate * (1.0 - sig))
    up_slope_ref[...] = silu


def partial_kernel(
    rows_ref, grads_ref, hidden_ref, gate_slope_ref, up_slope_ref, down_ref,
    part_ref, gate_pre_ref, up_pre_ref, score_ref, hidden_t,
):
    chunk = pl.program_id(0)
    width = rows_ref.shape[1]
    blocks = gate_pre_ref.shape[1] // width

    @pl.when(chunk == 0)
    def _():
        hidden_grad = dot(grads_ref[...], down_ref[...], LAST)
        hidden = hidden_ref[...]
        gate_pre_ref[...] = (hidden_grad * gate_slope_ref[...]).astype(BF16)
        up_pre_ref[...] = (hidden_grad * up_slope_ref[...]).astype(BF16)
        score = jnp.sum(hidden_grad * hidden.astype(F32), axis=1, keepdims=True)
        score_ref[...] = jnp.broadcast_to(score, score_ref.shape)
        hidden_t[...] = hidden.T

    rows_t = rows_ref[...].T
    for j in range(blocks):
        cols = slice(j * width, (j + 1) * width)
        part_ref[j] = dot(rows_t, gate_pre_ref[:, cols]).astype(BF16)
        part_ref[blocks + j] = dot(rows_t, up_pre_ref[:, cols]).astype(BF16)
    grads = grads_ref[:, pl.ds(pl.multiple_of(chunk * width, width), width)]
    for j in range(blocks):
        part_ref[2 * blocks + j] = dot(hidden_t[j * width : (j + 1) * width, :], grads).astype(BF16)


def return_kernel(hidden_ref, gate_pre_ref, up_pre_ref, down_ref, gate_ref, up_ref, out_ref, row_grad_ref):
    out_ref[...] = dot(hidden_ref[...], down_ref[...]).astype(BF16)
    row_grad_ref[...] = (
        dot(gate_pre_ref[...], gate_ref[...], LAST) + dot(up_pre_ref[...], up_ref[...], LAST)
    ).astype(BF16)


def combine_kernel(
    capacity, routes_ref, gates_ref, place_ref, score_ref, back_ref, back_grad_ref,
    out_ref, grad_ref, gates_grad_ref, high, low,
):
    @pl.when(pl.program_id(0) == 0)
    def _():
        routes_t, gates_t = routes_ref[...], gates_ref[...]
        place = place_ref[...].astype(F32)
        score = score_ref[:, 0:1] * place
        weight = jnp.zeros(place.shape, F32)
        for k, mask in enumerate(slot_masks(routes_t, place.shape[0], capacity)):
            weight = jnp.where(mask, gates_t[k : k + 1, :], weight)
            gates_grad_ref[k : k + 1, :] = (
                jnp.sum(jnp.where(mask, score, 0.0), axis=0, keepdims=True) / gates_t[k : k + 1, :]
            )
        weight = weight * place
        high[...] = weight.astype(BF16)
        low[...] = (weight - weight.astype(BF16).astype(F32)).astype(BF16)

    back = back_ref[...]
    out_ref[...] = (dot(high[...], back, FIRST) + dot(low[...], back, FIRST)).astype(BF16)
    grad_ref[...] = dot(place_ref[...], back_grad_ref[...], FIRST).astype(BF16)


def widen_kernel(part_ref, gate_ref, up_ref, down_ref):
    width = part_ref.shape[2]
    blocks = part_ref.shape[0] // 3
    for j in range(blocks):
        gate_ref[:, j * width : (j + 1) * width] = part_ref[j].astype(F32)
        up_ref[:, j * width : (j + 1) * width] = part_ref[blocks + j].astype(F32)
        down_ref[j * width : (j + 1) * width, :] = part_ref[2 * blocks + j].astype(F32)


def shape(dims, dtype=BF16):
    return jax.ShapeDtypeStruct(dims, dtype)


def whole(dims):
    return pl.BlockSpec(dims, lambda i: (0,) * len(dims))


def local(tokens, routes, gate_weights, w_gate, w_up, w_down, out_grad):
    count, top = routes.shape
    model = tokens.shape[1]
    experts = w_gate.shape[0] * lax.axis_size("expert")
    groups = lax.axis_size("dp")
    capacity = max(2, 4 * count * top // (3 * experts))
    slots = experts * capacity
    hid = w_gate.shape[2]
    width = model // groups
    blocks = hid // width
    w_gate, w_up, w_down = w_gate[0], w_up[0], w_down[0]
    routes_t, gates_t = routes.T, gate_weights.T

    send_rows, send_grads, place = pl.pallas_call(
        functools.partial(dispatch_kernel, capacity),
        out_shape=(shape((slots, model)), shape((slots, model)), shape((slots, count))),
        compiler_params=params(),
        cost_estimate=cost(4 * slots * count * model, 4 * slots * model),
        name="dispatch",
    )(routes_t, gates_t, tokens, out_grad)

    def exchange(array):
        wide = array.reshape(experts, capacity, array.shape[1])
        return lax.all_to_all(wide, "expert", 0, 0, tiled=True).reshape(array.shape)

    rows = exchange(send_rows)
    grads = exchange(send_grads)

    hidden, gate_slope, up_slope = pl.pallas_call(
        forward_kernel,
        grid=(blocks,),
        in_specs=[
            whole((slots, model)),
            pl.BlockSpec((model, width), lambda i: (0, i)),
            pl.BlockSpec((model, width), lambda i: (0, i)),
        ],
        out_specs=[pl.BlockSpec((slots, width), lambda i: (0, i))] * 3,
        out_shape=(shape((slots, hid)), shape((slots, hid), F32), shape((slots, hid), F32)),
        compiler_params=params(),
        cost_estimate=cost(4 * slots * model * hid, 2 * slots * model + 4 * model * hid + 10 * slots * hid),
        name="forward",
    )(rows, w_gate, w_up)

    part, gate_pre, up_pre, score = pl.pallas_call(
        partial_kernel,
        grid=(groups,),
        in_specs=[
            pl.BlockSpec((slots, width), lambda i: (0, i)),
            whole((slots, model)),
            whole((slots, hid)),
            whole((slots, hid)),
            whole((slots, hid)),
            whole((hid, model)),
        ],
        out_specs=[
            pl.BlockSpec((3 * blocks, width, width), lambda i: (i, 0, 0)),
            whole((slots, hid)),
            whole((slots, hid)),
            whole((slots, 128)),
        ],
        out_shape=(
            shape((groups * 3 * blocks, width, width)),
            shape((slots, hid)),
            shape((slots, hid)),
            shape((slots, 128), F32),
        ),
        scratch_shapes=[pltpu.VMEM((hid, slots), BF16)],
        compiler_params=params(),
        cost_estimate=cost(8 * slots * model * hid, 4 * slots * model + 8 * model * hid + 14 * slots * hid),
        name="partials",
    )(rows, grads, hidden, gate_slope, up_slope, w_down)

    summed = lax.psum_scatter(part, "dp", scatter_dimension=0, tiled=True)

    output, row_grad = pl.pallas_call(
        return_kernel,
        grid=(groups,),
        in_specs=[
            whole((slots, hid)),
            whole((slots, hid)),
            whole((slots, hid)),
            pl.BlockSpec((hid, width), lambda i: (0, i)),
            pl.BlockSpec((width, hid), lambda i: (i, 0)),
            pl.BlockSpec((width, hid), lambda i: (i, 0)),
        ],
        out_specs=[pl.BlockSpec((slots, width), lambda i: (0, i))] * 2,
        out_shape=(shape((slots, model)), shape((slots, model))),
        compiler_params=params(),
        cost_estimate=cost(6 * slots * model * hid, 4 * slots * model + 6 * model * hid + 6 * slots * hid),
        name="rows_back",
    )(hidden, gate_pre, up_pre, w_down, w_gate, w_up)

    back = exchange(output)
    back_grad = exchange(row_grad)
    back_score = exchange(score)

    half = model // 2
    layer_out, token_grad, gates_grad_t = pl.pallas_call(
        functools.partial(combine_kernel, capacity),
        grid=(2,),
        in_specs=[
            whole((top, count)),
            whole((top, count)),
            whole((slots, count)),
            whole((slots, 128)),
            pl.BlockSpec((slots, half), lambda i: (0, i)),
            pl.BlockSpec((slots, half), lambda i: (0, i)),
        ],
        out_specs=[
            pl.BlockSpec((count, half), lambda i: (0, i)),
            pl.BlockSpec((count, half), lambda i: (0, i)),
            whole((top, count)),
        ],
        out_shape=(shape((count, model)), shape((count, model)), shape((top, count), F32)),
        scratch_shapes=[pltpu.VMEM((slots, count), BF16)] * 2,
        compiler_params=params(),
        cost_estimate=cost(6 * slots * count * model, 4 * slots * model),
        name="combine",
    )(routes_t, gates_t, place, back_score, back, back_grad)

    gate_grad, up_grad, down_grad = pl.pallas_call(
        widen_kernel,
        out_shape=(shape((width, hid), F32), shape((width, hid), F32), shape((hid, width), F32)),
        compiler_params=params(),
        cost_estimate=cost(3 * width * hid, 18 * width * hid),
        name="widen",
    )(summed)
    return (layer_out, token_grad, gates_grad_t.T, gate_grad[None], up_grad[None], down_grad[None])


def solution(mesh):
    rows = P(("expert", "dp"), None)
    weights = P("expert", None, None)
    return jax.shard_map(
        local,
        mesh=mesh,
        in_specs=(rows, rows, rows, weights, weights, weights, rows),
        out_specs=(rows, rows, rows, P("expert", "dp", None), P("expert", "dp", None), P("expert", None, "dp")),
        check_vma=False,
    )
```

```python
import functools

import jax
import jax.numpy as jnp
from jax import lax
from jax.experimental import pallas as pl
from jax.experimental.pallas import tpu as pltpu
from jax.sharding import PartitionSpec as P

BF16 = jnp.bfloat16
F32 = jnp.float32
LAST = (((1,), (1,)), ((), ()))
FIRST = (((0,), (0,)), ((), ()))
VMEM_LIMIT = 60 * 2**20


def params():
    return pltpu.CompilerParams(vmem_limit_bytes=VMEM_LIMIT)


def cost(flops, nbytes, exps=0):
    return pl.CostEstimate(flops=flops, bytes_accessed=nbytes, transcendentals=exps)


def dot(a, b, dims=(((1,), (0,)), ((), ()))):
    return lax.dot_general(a, b, dims, preferred_element_type=F32)


def slot_masks(routes_t, slots, capacity):
    tokens = routes_t.shape[1]
    expert = lax.broadcasted_iota(jnp.int32, (slots, tokens), 0) // capacity
    return [expert == routes_t[k : k + 1, :] for k in range(routes_t.shape[0])]


def dispatch_kernel(capacity, routes_ref, gates_ref, tokens_ref, grads_ref, rows_ref, scaled_ref, place_ref):
    routes_t, gates_t = routes_ref[...], gates_ref[...]
    slots, tokens = place_ref.shape
    masks = slot_masks(routes_t, slots, capacity)
    hit = jnp.zeros((slots, tokens), F32)
    weight = jnp.zeros((slots, tokens), F32)
    for k, mask in enumerate(masks):
        hit = jnp.where(mask, 1.0, hit)
        weight = jnp.where(mask, gates_t[k : k + 1, :], weight)
    before = (
        lax.broadcasted_iota(jnp.int32, (tokens, tokens), 0)
        < lax.broadcasted_iota(jnp.int32, (tokens, tokens), 1)
    ).astype(F32).astype(BF16)
    rank = dot(hit.astype(BF16), before)
    mine = (lax.broadcasted_iota(jnp.int32, (slots, tokens), 0) % capacity).astype(F32)
    place = jnp.where(rank == mine, hit, 0.0)
    slot_weight = jnp.sum(place * weight, axis=1, keepdims=True)
    place_low = place.astype(BF16)
    place_ref[...] = place_low
    rows_ref[...] = dot(place_low, tokens_ref[...]).astype(BF16)
    scaled_ref[...] = (slot_weight * dot(place_low, grads_ref[...])).astype(BF16)


def forward_kernel(rows_ref, gate_ref, up_ref, hidden_ref, gate_slope_ref, up_slope_ref):
    rows = rows_ref[...]
    pre_gate = dot(rows, gate_ref[...])
    pre_up = dot(rows, up_ref[...])
    sig = jax.nn.sigmoid(pre_gate)
    silu = pre_gate * sig
    hidden_ref[...] = (silu * pre_up).astype(BF16)
    gate_slope_ref[...] = pre_up * sig * (1.0 + pre_gate * (1.0 - sig))
    up_slope_ref[...] = silu


def backward_kernel(
    grads_ref, hidden_ref, gate_slope_ref, up_slope_ref, down_ref, _, gate_pre_ref, up_pre_ref, hidden_t_ref
):
    hidden_grad = dot(grads_ref[...], down_ref[...], LAST)
    gate_pre_ref[...] = (hidden_grad * gate_slope_ref[...]).astype(BF16)
    up_pre_ref[...] = (hidden_grad * up_slope_ref[...]).astype(BF16)
    hidden_t_ref[...] = hidden_ref[...].T


def chunk_sums(rows_a, rows_b, grads_b, gate_pre, up_pre, hidden_t, held_a, held_b):
    width = rows_a.shape[1]
    blocks = gate_pre.shape[1] // width
    turned_a, turned_b = rows_a[...].T, rows_b[...].T
    grads = grads_b[...]
    for j in range(blocks + 1):
        source = gate_pre[:, j * width : (j + 1) * width] if j < blocks else up_pre[:, :width]
        total = dot(turned_a, source)
        for held in held_a:
            total = total + held[j].astype(F32)
        yield "a", j, total
    for j in range(2 * blocks - 1):
        if j < blocks - 1:
            total = dot(turned_b, up_pre[:, (j + 1) * width : (j + 2) * width])
        else:
            i = j - blocks + 1
            total = dot(hidden_t[i * width : (i + 1) * width, :], grads)
        for held in held_b:
            total = total + held[j].astype(F32)
        yield "b", j, total


def link_kernel(arrived, _, rows_a, rows_b, grads_b, gate_pre, up_pre, hidden_t, *refs):
    held_a, held_b = ([refs[0]], [refs[1]]) if arrived else ([], [])
    out = {"a": refs[-2], "b": refs[-1]}
    for part, j, total in chunk_sums(rows_a, rows_b, grads_b, gate_pre, up_pre, hidden_t, held_a, held_b):
        out[part][j] = total.astype(BF16)


def last_kernel(_, rows_a, rows_b, grads_b, gate_pre, up_pre, hidden_t, a0, a1, b0, b1, gate_ref, up_ref, down_ref):
    width = rows_a.shape[1]
    blocks = gate_pre.shape[1] // width
    for part, j, total in chunk_sums(rows_a, rows_b, grads_b, gate_pre, up_pre, hidden_t, [a0, a1], [b0, b1]):
        if part == "a" and j < blocks:
            gate_ref[:, j * width : (j + 1) * width] = total
        elif part == "a":
            up_ref[:, :width] = total
        elif j < blocks - 1:
            up_ref[:, (j + 1) * width : (j + 2) * width] = total
        else:
            i = j - blocks + 1
            down_ref[i * width : (i + 1) * width, :] = total


def output_kernel(hidden_ref, down_ref, out_ref):
    out_ref[...] = dot(hidden_ref[...], down_ref[...]).astype(BF16)


def row_grad_kernel(gate_pre_ref, up_pre_ref, gate_ref, up_ref, _, after, row_grad_ref):
    row_grad_ref[...] = (
        dot(gate_pre_ref[...], gate_ref[...], LAST) + dot(up_pre_ref[...], up_ref[...], LAST)
    ).astype(BF16)


def combine_kernel(
    capacity, routes_ref, gates_ref, place_ref, grads_ref, back_ref, back_grad_ref,
    out_ref, grad_ref, gates_grad_ref, high, low, score,
):
    step = pl.program_id(0)

    @pl.when(step == 0)
    def _():
        gates_t = gates_ref[...]
        weight = jnp.zeros(place_ref.shape, F32)
        for k, mask in enumerate(slot_masks(routes_ref[...], place_ref.shape[0], capacity)):
            weight = jnp.where(mask, gates_t[k : k + 1, :], weight)
        weight = weight * place_ref[...].astype(F32)
        high[...] = weight.astype(BF16)
        low[...] = (weight - weight.astype(BF16).astype(F32)).astype(BF16)
        score[...] = jnp.zeros_like(score)

    back = back_ref[...]
    out_ref[...] = (dot(high[...], back, FIRST) + dot(low[...], back, FIRST)).astype(BF16)
    grad_ref[...] = dot(place_ref[...], back_grad_ref[...], FIRST).astype(BF16)
    slot_grads = dot(place_ref[...], grads_ref[...])
    score[...] += jnp.sum(slot_grads * back.astype(F32), axis=1, keepdims=True)

    @pl.when(step == pl.num_programs(0) - 1)
    def _():
        placed = score[...] * place_ref[...].astype(F32)
        for k, mask in enumerate(slot_masks(routes_ref[...], place_ref.shape[0], capacity)):
            gates_grad_ref[k : k + 1, :] = jnp.sum(jnp.where(mask, placed, 0.0), axis=0, keepdims=True)


def shape(dims, dtype=BF16):
    return jax.ShapeDtypeStruct(dims, dtype)


def whole(dims):
    return pl.BlockSpec(dims, lambda i: (0,) * len(dims))


def local(tokens, routes, gate_weights, w_gate, w_up, w_down, out_grad):
    count, top = routes.shape
    model = tokens.shape[1]
    experts = w_gate.shape[0] * lax.axis_size("expert")
    groups = lax.axis_size("dp")
    capacity = max(2, 4 * count * top // (3 * experts))
    slots = experts * capacity
    hid = w_gate.shape[2]
    width = model // groups
    blocks = hid // width
    w_gate, w_up, w_down = w_gate[0], w_up[0], w_down[0]
    routes_t, gates_t = routes.T, gate_weights.T

    send_rows, send_grads, place = pl.pallas_call(
        functools.partial(dispatch_kernel, capacity),
        out_shape=(shape((slots, model)), shape((slots, model)), shape((slots, count))),
        compiler_params=params(),
        cost_estimate=cost(4 * slots * count * model, 4 * slots * model),
        name="dispatch",
    )(routes_t, gates_t, tokens, out_grad)

    def exchange(array):
        wide = array.reshape(experts, capacity, array.shape[1])
        return lax.all_to_all(wide, "expert", 0, 0, tiled=True).reshape(array.shape)

    rows = exchange(send_rows)
    grads = exchange(send_grads)

    hidden, gate_slope, up_slope = pl.pallas_call(
        forward_kernel,
        grid=(blocks,),
        in_specs=[
            whole((slots, model)),
            pl.BlockSpec((model, width), lambda i: (0, i)),
            pl.BlockSpec((model, width), lambda i: (0, i)),
        ],
        out_specs=[pl.BlockSpec((slots, width), lambda i: (0, i))] * 3,
        out_shape=(shape((slots, hid)), shape((slots, hid), F32), shape((slots, hid), F32)),
        compiler_params=params(),
        cost_estimate=cost(4 * slots * model * hid, 2 * slots * model + 4 * model * hid + 10 * slots * hid),
        name="forward",
    )(rows, w_gate, w_up)

    going_back = pl.pallas_call(
        output_kernel,
        grid=(groups,),
        in_specs=[whole((slots, hid)), pl.BlockSpec((hid, width), lambda i: (0, i))],
        out_specs=pl.BlockSpec((slots, width), lambda i: (0, i)),
        out_shape=shape((slots, 2 * model)),
        compiler_params=params(),
        cost_estimate=cost(2 * slots * model * hid, 2 * slots * model + 2 * model * hid + 2 * slots * hid),
        name="outputs",
    )(hidden, w_down)

    tile = pl.BlockSpec((slots, width), lambda i: (0, i))
    anywhere = pl.BlockSpec(memory_space=pl.ANY)
    gate_pre, up_pre, hidden_t = pl.pallas_call(
        backward_kernel,
        grid=(blocks,),
        in_specs=[whole((slots, model)), tile, tile, tile, pl.BlockSpec((width, model), lambda i: (i, 0)), anywhere],
        out_specs=[tile, tile, pl.BlockSpec((width, slots), lambda i: (i, 0))],
        out_shape=(shape((slots, hid)), shape((slots, hid)), shape((hid, slots))),
        compiler_params=params(),
        cost_estimate=cost(2 * slots * model * hid, 2 * slots * model + 2 * model * hid + 14 * slots * hid),
        name="backward",
    )(grads, hidden, gate_slope, up_slope, w_down, going_back)

    me = lax.axis_index("dp")
    place_of = me.reshape(1).astype(jnp.int32)

    def chain_call(kernel, step_a, step_b, out_shape, held, name, kept=(), after=()):
        size = lambda n: pl.BlockSpec((n, width, width), lambda i, p: (0, 0, 0))
        fixed = lambda dims: pl.BlockSpec(dims, lambda i, p: (0, 0))
        return pl.pallas_call(
            kernel,
            grid_spec=pltpu.PrefetchScalarGridSpec(
                num_scalar_prefetch=1,
                grid=(1,),
                in_specs=[
                    pl.BlockSpec((slots, width), lambda i, p: (0, lax.rem(p[0] + step_a, groups))),
                    pl.BlockSpec((slots, width), lambda i, p: (0, lax.rem(p[0] + step_b, groups))),
                    pl.BlockSpec((slots, width), lambda i, p: (0, lax.rem(p[0] + step_b, groups))),
                    fixed((slots, hid)),
                    fixed((slots, hid)),
                    fixed((hid, slots)),
                    *[size(h.shape[0]) for h in held],
                    *[anywhere for _ in (*kept, *after)],
                ],
                out_specs=[
                    *[anywhere for _ in kept],
                    *[pl.BlockSpec(o.shape, lambda i, p, n=len(o.shape): (0,) * n) for o in out_shape],
                ],
            ),
            out_shape=(*[shape(x.shape, x.dtype) for x in kept], *out_shape),
            input_output_aliases={7 + len(held) + i: i for i in range(len(kept))},
            compiler_params=params(),
            cost_estimate=cost(20 * 10**9, 60 * 2**20),
            name=name,
        )(place_of, rows, rows, grads, gate_pre, up_pre, hidden_t, *held, *kept, *after)

    up_ring = [(i, (i + 1) % groups) for i in range(groups)]
    down_ring = [(i, (i - 1) % groups) for i in range(groups)]
    part_shapes = (shape((blocks + 1, width, width)), shape((2 * blocks - 1, width, width)))
    half_way = groups // 2
    slots_of_ring = [(half_way, 0)] + [(k, s) for k in range(half_way - 1, 0, -1) for s in (1, 0)]
    def row_grads(after):
        return pl.pallas_call(
            row_grad_kernel,
            grid=(groups,),
            in_specs=[
                whole((slots, hid)),
                whole((slots, hid)),
                pl.BlockSpec((width, hid), lambda i: (i, 0)),
                pl.BlockSpec((width, hid), lambda i: (i, 0)),
                anywhere,
                anywhere,
            ],
            out_specs=pl.BlockSpec((slots, width), lambda i: (0, groups + i)),
            out_shape=shape((slots, 2 * model)),
            input_output_aliases={4: 0},
            compiler_params=params(),
            cost_estimate=cost(20 * 10**9, 60 * 2**20),
            name="row_grads",
        )(gate_pre, up_pre, w_gate, w_up, going_back, after)

    came, after = {}, ()
    for number, (k, swapped) in enumerate(slots_of_ring):
        step_a, step_b = (groups - k, k) if swapped else (k, groups - k)
        held = came.get((k, swapped), ())
        kept = (going_back,) if number == 2 else ()
        *kept, part_a, part_b = chain_call(
            functools.partial(link_kernel, bool(held)),
            step_a, step_b, part_shapes, held, f"chain_sum_{number}", kept, after,
        )
        after = (part_a,)
        if number == 1:
            going_back = row_grads(part_a)
            after = ()
        elif number == 2:
            [going_back] = kept
        ring_a, ring_b = (down_ring, up_ring) if swapped else (up_ring, down_ring)
        came[k - 1, swapped] = (lax.ppermute(part_a, "dp", ring_a), lax.ppermute(part_b, "dp", ring_b))

    back = exchange(going_back)

    half = model // 2
    layer_out, token_grad, gates_grad_t = pl.pallas_call(
        functools.partial(combine_kernel, capacity),
        grid=(2,),
        in_specs=[
            whole((top, count)),
            whole((top, count)),
            whole((slots, count)),
            pl.BlockSpec((count, half), lambda i: (0, i)),
            pl.BlockSpec((slots, half), lambda i: (0, i)),
            pl.BlockSpec((slots, half), lambda i: (0, 2 + i)),
        ],
        out_specs=[
            pl.BlockSpec((count, half), lambda i: (0, i)),
            pl.BlockSpec((count, half), lambda i: (0, i)),
            whole((top, count)),
        ],
        out_shape=(shape((count, model)), shape((count, model)), shape((top, count), F32)),
        scratch_shapes=[pltpu.VMEM((slots, count), BF16)] * 2 + [pltpu.VMEM((slots, 1), F32)],
        compiler_params=params(),
        cost_estimate=cost(8 * slots * count * model, 4 * slots * model),
        name="combine",
    )(routes_t, gates_t, place, out_grad, back, back)

    (a0, b0), (a1, b1) = came[0, 0], came[0, 1]
    gate_grad, up_grad, down_grad = chain_call(
        last_kernel,
        0,
        0,
        (shape((width, hid), F32), shape((width, hid), F32), shape((hid, width), F32)),
        (a0, a1, b0, b1),
        "chain_sum_last",
    )
    return (layer_out, token_grad, gates_grad_t.T, gate_grad[None], up_grad[None], down_grad[None])


def solution(mesh):
    rows = P(("expert", "dp"), None)
    weights = P("expert", None, None)
    return jax.shard_map(
        local,
        mesh=mesh,
        in_specs=(rows, rows, rows, weights, weights, weights, rows),
        out_specs=(rows, rows, rows, P("expert", "dp", None), P("expert", "dp", None), P("expert", None, "dp")),
        check_vma=False,
    )
```

```python
import functools

import jax
import jax.numpy as jnp
from jax import lax
from jax.experimental import pallas as pl
from jax.experimental.pallas import tpu as pltpu
from jax.sharding import PartitionSpec as P

BF16 = jnp.bfloat16
F32 = jnp.float32
LAST = (((1,), (1,)), ((), ()))
FIRST = (((0,), (0,)), ((), ()))


def params(mib=56):
    return pltpu.CompilerParams(vmem_limit_bytes=mib * 2**20)


def cost(flops, nbytes, exps=0):
    return pl.CostEstimate(flops=flops, bytes_accessed=nbytes, transcendentals=exps)


LONG = cost(20 * 10**9, 60 * 2**20)
SHORT = cost(1, 1)


def dot(a, b, dims=(((1,), (0,)), ((), ()))):
    return lax.dot_general(a, b, dims, preferred_element_type=F32)


def slot_masks(routes_t, slots, capacity):
    tokens = routes_t.shape[1]
    expert = lax.broadcasted_iota(jnp.int32, (slots, tokens), 0) // capacity
    return [expert == routes_t[k : k + 1, :] for k in range(routes_t.shape[0])]


def dispatch_kernel(capacity, routes_ref, gates_ref, tokens_ref, grads_ref, rows_ref, scaled_ref, place_ref):
    routes_t, gates_t = routes_ref[...], gates_ref[...]
    slots, tokens = place_ref.shape
    masks = slot_masks(routes_t, slots, capacity)
    hit = jnp.zeros((slots, tokens), F32)
    weight = jnp.zeros((slots, tokens), F32)
    for k, mask in enumerate(masks):
        hit = jnp.where(mask, 1.0, hit)
        weight = jnp.where(mask, gates_t[k : k + 1, :], weight)
    before = (
        lax.broadcasted_iota(jnp.int32, (tokens, tokens), 0)
        < lax.broadcasted_iota(jnp.int32, (tokens, tokens), 1)
    ).astype(F32).astype(BF16)
    rank = dot(hit.astype(BF16), before)
    mine = (lax.broadcasted_iota(jnp.int32, (slots, tokens), 0) % capacity).astype(F32)
    place = jnp.where(rank == mine, hit, 0.0)
    slot_weight = jnp.sum(place * weight, axis=1, keepdims=True)
    place_low = place.astype(BF16)
    place_ref[...] = place_low
    rows_ref[...] = dot(place_low, tokens_ref[...]).astype(BF16)
    scaled_ref[...] = (slot_weight * dot(place_low, grads_ref[...])).astype(BF16)


def forward_kernel(rows_ref, gate_ref, up_ref, hidden_ref, gate_slope_ref, up_slope_ref):
    rows = rows_ref[...]
    pre_gate = dot(rows, gate_ref[...])
    pre_up = dot(rows, up_ref[...])
    sig = jax.nn.sigmoid(pre_gate)
    silu = pre_gate * sig
    hidden_ref[...] = (silu * pre_up).astype(BF16)
    gate_slope_ref[...] = pre_up * sig * (1.0 + pre_gate * (1.0 - sig))
    up_slope_ref[...] = silu


def backward_kernel(
    grads_ref, hidden_ref, gate_slope_ref, up_slope_ref, down_ref, _, gate_pre_ref, up_pre_ref, hidden_t_ref
):
    hidden_grad = dot(grads_ref[...], down_ref[...], LAST)
    gate_pre_ref[...] = (hidden_grad * gate_slope_ref[...]).astype(BF16)
    up_pre_ref[...] = (hidden_grad * up_slope_ref[...]).astype(BF16)
    hidden_t_ref[...] = hidden_ref[...].T


def chunk_sums(step_a, step_b, groups, me_ref, rows, grads, gate_pre, up_pre, hidden_t, held_a=(), held_b=()):
    width = rows.shape[1] // groups
    blocks = gate_pre.shape[1] // width
    me = me_ref[0]

    def columns(step):
        return pl.ds(pl.multiple_of(lax.rem(me + step, groups) * width, width), width)

    turned_a = rows[:, columns(step_a)].T
    for j in range(blocks + 1):
        source = gate_pre[:, j * width : (j + 1) * width] if j < blocks else up_pre[:, :width]
        total = dot(turned_a, source)
        for held in held_a:
            total = total + held[j].astype(F32)
        yield "a", j, total
    turned_b = turned_a if step_a == step_b else rows[:, columns(step_b)].T
    grads_b = grads[:, columns(step_b)]
    for j in range(2 * blocks - 1):
        if j < blocks - 1:
            total = dot(turned_b, up_pre[:, (j + 1) * width : (j + 2) * width])
        else:
            i = j - blocks + 1
            total = dot(hidden_t[i * width : (i + 1) * width, :], grads_b)
        for held in held_b:
            total = total + held[j].astype(F32)
        yield "b", j, total


def link_kernel(step_a, step_b, groups, arrived, me_ref, *refs):
    held = [[refs[5]], [refs[6]]] if arrived else []
    out = {"a": refs[-2], "b": refs[-1]}
    for part, j, total in chunk_sums(step_a, step_b, groups, me_ref, *refs[:5], *held):
        out[part][j] = total.astype(out[part].dtype)


def last_kernel(own_a, own_b, a0, b0, _, gate_ref, up_ref, down_ref):
    width = own_a.shape[1]
    blocks = own_a.shape[0] - 1
    for j in range(blocks):
        gate_ref[:, j * width : (j + 1) * width] = own_a[j] + a0[j].astype(F32)
        down_ref[j * width : (j + 1) * width, :] = own_b[blocks - 1 + j] + b0[blocks - 1 + j].astype(F32)
    up_ref[:, :width] = own_a[blocks] + a0[blocks].astype(F32)
    for j in range(blocks - 1):
        up_ref[:, (j + 1) * width : (j + 2) * width] = own_b[j] + b0[j].astype(F32)


def output_kernel(hidden_ref, down_ref, out_ref, token_ref):
    token_ref[...] = jnp.zeros_like(token_ref)
    out_ref[...] = dot(hidden_ref[...], down_ref[...]).astype(BF16)


def row_grad_kernel(gate_pre_ref, up_pre_ref, gate_ref, up_ref, _, after, row_grad_ref, token_ref):
    token_ref[...] = jnp.zeros_like(token_ref)
    row_grad_ref[...] = (
        dot(gate_pre_ref[...], gate_ref[...], LAST) + dot(up_pre_ref[...], up_ref[...], LAST)
    ).astype(BF16)


def combine_kernel(
    capacity, routes_ref, gates_ref, place_ref, grads_ref, back_ref, back_grad_ref,
    out_ref, grad_ref, gates_grad_ref, high, low, score,
):
    step = pl.program_id(0)

    @pl.when(step == 0)
    def _():
        gates_t = gates_ref[...]
        weight = jnp.zeros(place_ref.shape, F32)
        for k, mask in enumerate(slot_masks(routes_ref[...], place_ref.shape[0], capacity)):
            weight = jnp.where(mask, gates_t[k : k + 1, :], weight)
        weight = weight * place_ref[...].astype(F32)
        high[...] = weight.astype(BF16)
        low[...] = (weight - weight.astype(BF16).astype(F32)).astype(BF16)
        score[...] = jnp.zeros_like(score)

    back = back_ref[...]
    out_ref[...] = (dot(high[...], back, FIRST) + dot(low[...], back, FIRST)).astype(BF16)
    grad_ref[...] = dot(place_ref[...], back_grad_ref[...], FIRST).astype(BF16)
    slot_grads = dot(place_ref[...], grads_ref[...])
    score[...] += jnp.sum(slot_grads * back.astype(F32), axis=1, keepdims=True)

    @pl.when(step == pl.num_programs(0) - 1)
    def _():
        placed = score[...] * place_ref[...].astype(F32)
        for k, mask in enumerate(slot_masks(routes_ref[...], place_ref.shape[0], capacity)):
            gates_grad_ref[k : k + 1, :] = jnp.sum(jnp.where(mask, placed, 0.0), axis=0, keepdims=True)


def shape(dims, dtype=BF16):
    return jax.ShapeDtypeStruct(dims, dtype)


def whole(dims):
    return pl.BlockSpec(dims, lambda i: (0,) * len(dims))


def local(tokens, routes, gate_weights, w_gate, w_up, w_down, out_grad):
    count, top = routes.shape
    model = tokens.shape[1]
    experts = w_gate.shape[0] * lax.axis_size("expert")
    groups = lax.axis_size("dp")
    capacity = max(2, 4 * count * top // (3 * experts))
    slots = experts * capacity
    hid = w_gate.shape[2]
    width = model // groups
    blocks = hid // width
    w_gate, w_up, w_down = w_gate[0], w_up[0], w_down[0]
    routes_t, gates_t = routes.T, gate_weights.T

    send_rows, send_grads, place = pl.pallas_call(
        functools.partial(dispatch_kernel, capacity),
        out_shape=(shape((slots, model)), shape((slots, model)), shape((slots, count))),
        compiler_params=params(),
        cost_estimate=cost(4 * slots * count * model, 4 * slots * model),
        name="dispatch",
    )(routes_t, gates_t, tokens, out_grad)

    def exchange(array):
        wide = array.reshape(experts, capacity, array.shape[1])
        return lax.all_to_all(wide, "expert", 0, 0, tiled=True).reshape(array.shape)

    rows = exchange(send_rows)
    grads = exchange(send_grads)

    hidden, gate_slope, up_slope = pl.pallas_call(
        forward_kernel,
        grid=(blocks,),
        in_specs=[
            whole((slots, model)),
            pl.BlockSpec((model, width), lambda i: (0, i)),
            pl.BlockSpec((model, width), lambda i: (0, i)),
        ],
        out_specs=[pl.BlockSpec((slots, width), lambda i: (0, i))] * 3,
        out_shape=(shape((slots, hid)), shape((slots, hid), F32), shape((slots, hid), F32)),
        compiler_params=params(),
        cost_estimate=cost(4 * slots * model * hid, 2 * slots * model + 4 * model * hid + 10 * slots * hid),
        name="forward",
    )(rows, w_gate, w_up)

    going_back, token = pl.pallas_call(
        output_kernel,
        grid=(groups,),
        in_specs=[whole((slots, hid)), pl.BlockSpec((hid, width), lambda i: (0, i))],
        out_specs=[pl.BlockSpec((slots, width), lambda i: (0, i)), whole((8, 128))],
        out_shape=(shape((slots, 2 * model)), shape((8, 128), F32)),
        compiler_params=params(),
        cost_estimate=cost(2 * slots * model * hid, 2 * slots * model + 2 * model * hid + 2 * slots * hid),
        name="outputs",
    )(hidden, w_down)

    tile = pl.BlockSpec((slots, width), lambda i: (0, i))
    anywhere = pl.BlockSpec(memory_space=pltpu.HBM)
    gate_pre, up_pre, hidden_t = pl.pallas_call(
        backward_kernel,
        grid=(blocks,),
        in_specs=[pl.BlockSpec(memory_space=pltpu.VMEM), tile, tile, tile, pl.BlockSpec((width, model), lambda i: (i, 0)), anywhere],
        out_specs=[tile, tile, pl.BlockSpec((width, slots), lambda i: (i, 0))],
        out_shape=(shape((slots, hid)), shape((slots, hid)), shape((hid, slots))),
        compiler_params=params(36),
        cost_estimate=cost(2 * slots * model * hid, 2 * slots * model + 2 * model * hid + 14 * slots * hid),
        name="backward",
    )(grads, hidden, gate_slope, up_slope, w_down, token)

    me = lax.axis_index("dp")
    place_of = me.reshape(1).astype(jnp.int32)

    resident = pl.BlockSpec(memory_space=pltpu.VMEM)

    def chain_call(step_a, step_b, dtype, held, name, after):
        parts = (shape((blocks + 1, width, width), dtype), shape((2 * blocks - 1, width, width), dtype))
        return pl.pallas_call(
            functools.partial(link_kernel, step_a, step_b, groups, bool(held)),
            in_specs=[
                pl.BlockSpec(memory_space=pltpu.SMEM),
                *[resident] * (5 + len(held)),
                *[anywhere] * len(after),
            ],
            out_specs=[resident, resident],
            out_shape=parts,
            compiler_params=params(16),
            cost_estimate=LONG,
            name=name,
        )(place_of, rows, grads, gate_pre, up_pre, hidden_t, *held, *after)

    up_ring = [(i, (i + 1) % groups) for i in range(groups)]
    down_ring = [(i, (i - 1) % groups) for i in range(groups)]
    half_way = groups // 2
    slots_of_ring = [(half_way, 0)] + [(k, s) for k in range(half_way - 1, 0, -1) for s in (1, 0)]
    def row_grads(after):
        return pl.pallas_call(
            row_grad_kernel,
            grid=(groups,),
            in_specs=[
                whole((slots, hid)),
                whole((slots, hid)),
                pl.BlockSpec((width, hid), lambda i: (i, 0)),
                pl.BlockSpec((width, hid), lambda i: (i, 0)),
                anywhere,
                anywhere,
            ],
            out_specs=[pl.BlockSpec((slots, width), lambda i: (0, groups + i)), whole((8, 128))],
            out_shape=(shape((slots, 2 * model)), shape((8, 128), F32)),
            input_output_aliases={4: 0},
            compiler_params=params(52),
            cost_estimate=SHORT,
            name="row_grads",
        )(gate_pre, up_pre, w_gate, w_up, going_back, after)

    came, after = {}, ()
    for number, (k, swapped) in enumerate(slots_of_ring):
        step_a, step_b = (groups - k, k) if swapped else (k, groups - k)
        held = came.get((k, swapped), ())
        part_a, part_b = chain_call(step_a, step_b, BF16, held, f"chain_sum_{number}", after)
        after = (part_a,)
        if number == 1:
            going_back, token = row_grads(part_a)
            after = (token,)
        ring_a, ring_b = (down_ring, up_ring) if swapped else (up_ring, down_ring)
        came[k - 1, swapped] = (lax.ppermute(part_a, "dp", ring_a), lax.ppermute(part_b, "dp", ring_b))

    back = exchange(going_back)

    half = model // 2
    layer_out, token_grad, gates_grad_t = pl.pallas_call(
        functools.partial(combine_kernel, capacity),
        grid=(2,),
        in_specs=[
            whole((top, count)),
            whole((top, count)),
            whole((slots, count)),
            pl.BlockSpec((count, half), lambda i: (0, i)),
            pl.BlockSpec((slots, half), lambda i: (0, i)),
            pl.BlockSpec((slots, half), lambda i: (0, 2 + i)),
        ],
        out_specs=[
            pl.BlockSpec((count, half), lambda i: (0, i)),
            pl.BlockSpec((count, half), lambda i: (0, i)),
            whole((top, count)),
        ],
        out_shape=(shape((count, model)), shape((count, model)), shape((top, count), F32)),
        scratch_shapes=[pltpu.VMEM((slots, count), BF16)] * 2 + [pltpu.VMEM((slots, 1), F32)],
        compiler_params=params(),
        cost_estimate=cost(8 * slots * count * model, 4 * slots * model),
        name="combine",
    )(routes_t, gates_t, place, out_grad, back, back)

    own_a, own_b = chain_call(0, 0, F32, came[0, 1], "chain_sum_own", after)
    gate_grad, up_grad, down_grad = pl.pallas_call(
        last_kernel,
        in_specs=[*[resident] * 4, anywhere],
        out_shape=(shape((width, hid), F32), shape((width, hid), F32), shape((hid, width), F32)),
        compiler_params=params(16),
        cost_estimate=SHORT,
        name="chain_sum_last",
    )(own_a, own_b, *came[0, 0], token_grad)
    return (layer_out, token_grad, gates_grad_t.T, gate_grad[None], up_grad[None], down_grad[None])


def solution(mesh):
    rows = P(("expert", "dp"), None)
    weights = P("expert", None, None)
    return jax.shard_map(
        local,
        mesh=mesh,
        in_specs=(rows, rows, rows, weights, weights, weights, rows),
        out_specs=(rows, rows, rows, P("expert", "dp", None), P("expert", "dp", None), P("expert", None, "dp")),
        check_vma=False,
    )
```

```python
import functools

import jax
import jax.numpy as jnp
from jax import lax
from jax.experimental import pallas as pl
from jax.experimental.pallas import tpu as pltpu
from jax.sharding import PartitionSpec as P

BF16 = jnp.bfloat16
F32 = jnp.float32
LAST = (((1,), (1,)), ((), ()))
FIRST = (((0,), (0,)), ((), ()))


def params(mib=16):
    return pltpu.CompilerParams(vmem_limit_bytes=mib * 2**20)


def cost(flops, nbytes, exps=0):
    return pl.CostEstimate(flops=flops, bytes_accessed=nbytes, transcendentals=exps)


LONG = cost(20 * 10**9, 60 * 2**20)
SHORT = cost(1, 1)


def dot(a, b, dims=(((1,), (0,)), ((), ()))):
    return lax.dot_general(a, b, dims, preferred_element_type=F32)


def slot_masks(routes_t, slots, capacity):
    tokens = routes_t.shape[1]
    expert = lax.broadcasted_iota(jnp.int32, (slots, tokens), 0) // capacity
    return [expert == routes_t[k : k + 1, :] for k in range(routes_t.shape[0])]


def dispatch_kernel(capacity, routes_ref, gates_ref, tokens_ref, grads_ref, wide_ref, place_ref):
    routes_t, gates_t = routes_ref[...], gates_ref[...]
    slots, tokens = place_ref.shape
    masks = slot_masks(routes_t, slots, capacity)
    hit = jnp.zeros((slots, tokens), F32)
    weight = jnp.zeros((slots, tokens), F32)
    for k, mask in enumerate(masks):
        hit = jnp.where(mask, 1.0, hit)
        weight = jnp.where(mask, gates_t[k : k + 1, :], weight)
    before = (
        lax.broadcasted_iota(jnp.int32, (tokens, tokens), 0)
        < lax.broadcasted_iota(jnp.int32, (tokens, tokens), 1)
    ).astype(F32).astype(BF16)
    rank = dot(hit.astype(BF16), before)
    mine = (lax.broadcasted_iota(jnp.int32, (slots, tokens), 0) % capacity).astype(F32)
    place = jnp.where(rank == mine, hit, 0.0)
    slot_weight = jnp.sum(place * weight, axis=1, keepdims=True)
    place_low = place.astype(BF16)
    place_ref[...] = place_low
    model = tokens_ref.shape[1]
    wide_ref[:, :model] = dot(place_low, tokens_ref[...]).astype(BF16)
    wide_ref[:, model:] = (slot_weight * dot(place_low, grads_ref[...])).astype(BF16)


def expert_kernel(width, wide_ref, gate_ref, up_ref, down_ref, hidden_ref, hidden_t_ref, gate_pre_ref, up_pre_ref):
    model, hid = gate_ref.shape
    for j in range(hid // width):
        cols = slice(j * width, (j + 1) * width)
        pre_gate = dot(wide_ref[:, :model], gate_ref[:, cols])
        pre_up = dot(wide_ref[:, :model], up_ref[:, cols])
        hidden_grad = dot(wide_ref[:, model:], down_ref[cols, :], LAST)
        sig = jax.nn.sigmoid(pre_gate)
        silu = pre_gate * sig
        hidden = (silu * pre_up).astype(BF16)
        hidden_ref[:, cols] = hidden
        hidden_t_ref[cols, :] = hidden.T
        gate_pre_ref[:, cols] = (hidden_grad * pre_up * sig * (1.0 + pre_gate * (1.0 - sig))).astype(BF16)
        up_pre_ref[:, cols] = (hidden_grad * silu).astype(BF16)


def chunk_sums(step_a, step_b, groups, me_ref, wide, gate_pre, up_pre, hidden_t, held_a=(), held_b=()):
    model = wide.shape[1] // 2
    width = model // groups
    blocks = gate_pre.shape[1] // width
    me = me_ref[0]

    def columns(step, first=0):
        return pl.ds(pl.multiple_of(first + lax.rem(me + step, groups) * width, width), width)

    turned_a = wide[:, columns(step_a)].T
    for j in range(blocks + 1):
        source = gate_pre[:, j * width : (j + 1) * width] if j < blocks else up_pre[:, :width]
        total = dot(turned_a, source)
        for held in held_a:
            total = total + held[j].astype(F32)
        yield "a", j, total
    turned_b = turned_a if step_a == step_b else wide[:, columns(step_b)].T
    grads_b = wide[:, columns(step_b, model)]
    for j in range(2 * blocks - 1):
        if j < blocks - 1:
            total = dot(turned_b, up_pre[:, (j + 1) * width : (j + 2) * width])
        else:
            i = j - blocks + 1
            total = dot(hidden_t[i * width : (i + 1) * width, :], grads_b)
        for held in held_b:
            total = total + held[j].astype(F32)
        yield "b", j, total


def link_kernel(step_a, step_b, groups, arrived, me_ref, *refs):
    held = [[refs[4]], [refs[5]]] if arrived else []
    out = {"a": refs[-2], "b": refs[-1]}
    for part, j, total in chunk_sums(step_a, step_b, groups, me_ref, *refs[:4], *held):
        out[part][j] = total.astype(out[part].dtype)


def last_kernel(own_a, own_b, a0, b0, gate_ref, up_ref, down_ref):
    width = own_a.shape[1]
    blocks = own_a.shape[0] - 1
    for j in range(blocks):
        gate_ref[:, j * width : (j + 1) * width] = own_a[j] + a0[j].astype(F32)
        down_ref[j * width : (j + 1) * width, :] = own_b[blocks - 1 + j] + b0[blocks - 1 + j].astype(F32)
    up_ref[:, :width] = own_a[blocks] + a0[blocks].astype(F32)
    for j in range(blocks - 1):
        up_ref[:, (j + 1) * width : (j + 2) * width] = own_b[j] + b0[j].astype(F32)


def back_kernel(width, hidden_ref, gate_pre_ref, up_pre_ref, down_ref, gate_ref, up_ref, _, back_ref, token_ref):
    token_ref[...] = jnp.zeros_like(token_ref)
    model = down_ref.shape[1]
    for j in range(model // width):
        cols = slice(j * width, (j + 1) * width)
        back_ref[:, cols] = dot(hidden_ref[...], down_ref[:, cols]).astype(BF16)
        row_grad = dot(gate_pre_ref[...], gate_ref[cols, :], LAST) + dot(up_pre_ref[...], up_ref[cols, :], LAST)
        back_ref[:, model + j * width : model + (j + 1) * width] = row_grad.astype(BF16)


def combine_kernel(
    capacity, routes_ref, gates_ref, place_ref, grads_ref, back_ref, back_grad_ref,
    out_ref, grad_ref, gates_grad_ref, high, low, score,
):
    step = pl.program_id(0)

    @pl.when(step == 0)
    def _():
        gates_t = gates_ref[...]
        weight = jnp.zeros(place_ref.shape, F32)
        for k, mask in enumerate(slot_masks(routes_ref[...], place_ref.shape[0], capacity)):
            weight = jnp.where(mask, gates_t[k : k + 1, :], weight)
        weight = weight * place_ref[...].astype(F32)
        high[...] = weight.astype(BF16)
        low[...] = (weight - weight.astype(BF16).astype(F32)).astype(BF16)
        score[...] = jnp.zeros_like(score)

    back = back_ref[...]
    out_ref[...] = (dot(high[...], back, FIRST) + dot(low[...], back, FIRST)).astype(BF16)
    grad_ref[...] = dot(place_ref[...], back_grad_ref[...], FIRST).astype(BF16)
    slot_grads = dot(place_ref[...], grads_ref[...])
    score[...] += jnp.sum(slot_grads * back.astype(F32), axis=1, keepdims=True)

    @pl.when(step == pl.num_programs(0) - 1)
    def _():
        placed = score[...] * place_ref[...].astype(F32)
        for k, mask in enumerate(slot_masks(routes_ref[...], place_ref.shape[0], capacity)):
            gates_grad_ref[k : k + 1, :] = jnp.sum(jnp.where(mask, placed, 0.0), axis=0, keepdims=True)


def shape(dims, dtype=BF16):
    return jax.ShapeDtypeStruct(dims, dtype)


def whole(dims):
    return pl.BlockSpec(dims, lambda i: (0,) * len(dims))


def local(tokens, routes, gate_weights, w_gate, w_up, w_down, out_grad):
    count, top = routes.shape
    model = tokens.shape[1]
    experts = w_gate.shape[0] * lax.axis_size("expert")
    groups = lax.axis_size("dp")
    capacity = max(2, 4 * count * top // (3 * experts))
    slots = experts * capacity
    hid = w_gate.shape[2]
    width = model // groups
    blocks = hid // width
    w_gate, w_up, w_down = w_gate[0], w_up[0], w_down[0]
    routes_t, gates_t = routes.T, gate_weights.T

    resident = pl.BlockSpec(memory_space=pltpu.VMEM)
    anywhere = pl.BlockSpec(memory_space=pl.ANY)
    send, place = pl.pallas_call(
        functools.partial(dispatch_kernel, capacity),
        in_specs=[resident] * 4,
        out_specs=[resident] * 2,
        out_shape=(shape((slots, 2 * model)), shape((slots, count))),
        compiler_params=params(),
        cost_estimate=cost(4 * slots * count * model, 4 * slots * model),
        name="dispatch",
    )(routes_t, gates_t, tokens, out_grad)

    def exchange(array):
        wide = array.reshape(experts, capacity, array.shape[1])
        return lax.all_to_all(wide, "expert", 0, 0, tiled=True).reshape(array.shape)

    wide = exchange(send)
    hidden, hidden_t, gate_pre, up_pre = pl.pallas_call(
        functools.partial(expert_kernel, width),
        in_specs=[resident] * 4,
        out_specs=[resident] * 4,
        out_shape=(shape((slots, hid)), shape((hid, slots)), shape((slots, hid)), shape((slots, hid))),
        compiler_params=params(),
        cost_estimate=cost(6 * slots * model * hid, 4 * slots * model + 6 * model * hid + 8 * slots * hid),
        name="expert",
    )(wide, w_gate, w_up, w_down)

    me = lax.axis_index("dp")
    place_of = me.reshape(1).astype(jnp.int32)

    def chain_call(step_a, step_b, dtype, held, name, after):
        parts = (shape((blocks + 1, width, width), dtype), shape((2 * blocks - 1, width, width), dtype))
        return pl.pallas_call(
            functools.partial(link_kernel, step_a, step_b, groups, bool(held)),
            in_specs=[
                pl.BlockSpec(memory_space=pltpu.SMEM),
                *[resident] * (4 + len(held)),
                *[anywhere] * len(after),
            ],
            out_specs=[resident, resident],
            out_shape=parts,
            compiler_params=params(),
            cost_estimate=LONG,
            name=name,
        )(place_of, wide, gate_pre, up_pre, hidden_t, *held, *after)

    up_ring = [(i, (i + 1) % groups) for i in range(groups)]
    down_ring = [(i, (i - 1) % groups) for i in range(groups)]
    half_way = groups // 2
    slots_of_ring = [(half_way, 0)] + [(k, s) for k in range(half_way - 1, 0, -1) for s in (1, 0)]
    def rows_back(after):
        return pl.pallas_call(
            functools.partial(back_kernel, width),
            in_specs=[*[resident] * 6, anywhere],
            out_specs=[resident] * 2,
            out_shape=(shape((slots, 2 * model)), shape((8, 128), F32)),
            compiler_params=params(),
            cost_estimate=SHORT,
            name="rows_back",
        )(hidden, gate_pre, up_pre, w_down, w_gate, w_up, after)

    came, after = {}, ()
    for number, (k, swapped) in enumerate(slots_of_ring):
        step_a, step_b = (groups - k, k) if swapped else (k, groups - k)
        held = came.get((k, swapped), ())
        part_a, part_b = chain_call(step_a, step_b, BF16, held, f"chain_sum_{number}", after)
        after = (part_a,)
        if number == 1:
            going_back, token = rows_back(part_a)
            after = (token,)
        ring_a, ring_b = (down_ring, up_ring) if swapped else (up_ring, down_ring)
        came[k - 1, swapped] = (lax.ppermute(part_a, "dp", ring_a), lax.ppermute(part_b, "dp", ring_b))

    back = exchange(going_back)

    half = model // 2
    layer_out, token_grad, gates_grad_t = pl.pallas_call(
        functools.partial(combine_kernel, capacity),
        grid=(2,),
        in_specs=[
            whole((top, count)),
            whole((top, count)),
            whole((slots, count)),
            pl.BlockSpec((count, half), lambda i: (0, i)),
            pl.BlockSpec((slots, half), lambda i: (0, i)),
            pl.BlockSpec((slots, half), lambda i: (0, 2 + i)),
        ],
        out_specs=[
            pl.BlockSpec((count, half), lambda i: (0, i)),
            pl.BlockSpec((count, half), lambda i: (0, i)),
            whole((top, count)),
        ],
        out_shape=(shape((count, model)), shape((count, model)), shape((top, count), F32)),
        scratch_shapes=[pltpu.VMEM((slots, count), BF16)] * 2 + [pltpu.VMEM((slots, 1), F32)],
        compiler_params=params(),
        cost_estimate=cost(8 * slots * count * model, 4 * slots * model),
        name="combine",
    )(routes_t, gates_t, place, out_grad, back, back)

    own_a, own_b = chain_call(0, 0, F32, came[0, 1], "chain_sum_own", (*after, token_grad))
    gate_grad, up_grad, down_grad = pl.pallas_call(
        last_kernel,
        in_specs=[resident] * 4,
        out_shape=(shape((width, hid), F32), shape((width, hid), F32), shape((hid, width), F32)),
        compiler_params=params(),
        cost_estimate=SHORT,
        name="chain_sum_last",
    )(own_a, own_b, *came[0, 0])
    return (layer_out, token_grad, gates_grad_t.T, gate_grad[None], up_grad[None], down_grad[None])


def solution(mesh):
    rows = P(("expert", "dp"), None)
    weights = P("expert", None, None)
    return jax.shard_map(
        local,
        mesh=mesh,
        in_specs=(rows, rows, rows, weights, weights, weights, rows),
        out_specs=(rows, rows, rows, P("expert", "dp", None), P("expert", "dp", None), P("expert", None, "dp")),
        check_vma=False,
    )
```

```python
import functools

import jax
import jax.numpy as jnp
from jax import lax
from jax.experimental import pallas as pl
from jax.experimental.pallas import tpu as pltpu
from jax.sharding import PartitionSpec as P

BF16 = jnp.bfloat16
F32 = jnp.float32
LAST = (((1,), (1,)), ((), ()))
FIRST = (((0,), (0,)), ((), ()))


def params(mib=16):
    return pltpu.CompilerParams(vmem_limit_bytes=mib * 2**20)


def cost(flops, nbytes, exps=0):
    return pl.CostEstimate(flops=flops, bytes_accessed=nbytes, transcendentals=exps)


LONG = cost(20 * 10**9, 60 * 2**20)
SHORT = cost(1, 1)


def dot(a, b, dims=(((1,), (0,)), ((), ()))):
    return lax.dot_general(a, b, dims, preferred_element_type=F32)


def slot_masks(routes_t, slots, capacity):
    tokens = routes_t.shape[1]
    expert = lax.broadcasted_iota(jnp.int32, (slots, tokens), 0) // capacity
    return [expert == routes_t[k : k + 1, :] for k in range(routes_t.shape[0])]


def dispatch_kernel(capacity, routes_ref, gates_ref, tokens_ref, grads_ref, wide_ref, place_ref, slot_weight):
    step, half = pl.program_id(0), pl.num_programs(0) // 2

    @pl.when(step == 0)
    def _():
        slots, tokens = place_ref.shape
        hit = jnp.zeros((slots, tokens), F32)
        weight = jnp.zeros((slots, tokens), F32)
        gates_t = gates_ref[...]
        for k, mask in enumerate(slot_masks(routes_ref[...], slots, capacity)):
            hit = jnp.where(mask, 1.0, hit)
            weight = jnp.where(mask, gates_t[k : k + 1, :], weight)
        before = (
            lax.broadcasted_iota(jnp.int32, (tokens, tokens), 0)
            < lax.broadcasted_iota(jnp.int32, (tokens, tokens), 1)
        ).astype(F32).astype(BF16)
        rank = dot(hit.astype(BF16), before)
        mine = (lax.broadcasted_iota(jnp.int32, (slots, tokens), 0) % capacity).astype(F32)
        place = jnp.where(rank == mine, hit, 0.0)
        slot_weight[...] = jnp.sum(place * weight, axis=1, keepdims=True)
        place_ref[...] = place.astype(BF16)

    @pl.when(step < half)
    def _():
        wide_ref[...] = dot(place_ref[...], tokens_ref[...]).astype(BF16)

    @pl.when(step >= half)
    def _():
        wide_ref[...] = (slot_weight[...] * dot(place_ref[...], grads_ref[...])).astype(BF16)


def expert_kernel(rows_ref, grads_ref, gate_ref, up_ref, down_ref, hidden_ref, hidden_t_ref, gate_pre_ref, up_pre_ref):
    rows = rows_ref[...]
    pre_gate = dot(rows, gate_ref[...])
    pre_up = dot(rows, up_ref[...])
    hidden_grad = dot(grads_ref[...], down_ref[...], LAST)
    sig = jax.nn.sigmoid(pre_gate)
    silu = pre_gate * sig
    hidden = (silu * pre_up).astype(BF16)
    hidden_ref[...] = hidden
    hidden_t_ref[...] = hidden.T
    gate_pre_ref[...] = (hidden_grad * pre_up * sig * (1.0 + pre_gate * (1.0 - sig))).astype(BF16)
    up_pre_ref[...] = (hidden_grad * silu).astype(BF16)


def chunk_sums(rows_a, rows_b, grads_b, gate_pre, up_pre, hidden_t, held_a=(), held_b=()):
    width = rows_a.shape[1]
    blocks = gate_pre.shape[1] // width
    turned_a, turned_b, grads = rows_a[...].T, rows_b[...].T, grads_b[...]
    for j in range(blocks + 1):
        source = gate_pre[:, j * width : (j + 1) * width] if j < blocks else up_pre[:, :width]
        total = dot(turned_a, source)
        for held in held_a:
            total = total + held[j].astype(F32)
        yield "a", j, total
    for j in range(2 * blocks - 1):
        if j < blocks - 1:
            total = dot(turned_b, up_pre[:, (j + 1) * width : (j + 2) * width])
        else:
            i = j - blocks + 1
            total = dot(hidden_t[i * width : (i + 1) * width, :], grads)
        for held in held_b:
            total = total + held[j].astype(F32)
        yield "b", j, total


def link_kernel(arrived, _, *refs):
    held = [[refs[6]], [refs[7]]] if arrived else []
    out = {"a": refs[-2], "b": refs[-1]}
    for part, j, total in chunk_sums(*refs[:6], *held):
        out[part][j] = total.astype(out[part].dtype)


def last_kernel(own_a, own_b, a0, b0, gate_ref, up_ref, down_ref):
    width = own_a.shape[1]
    blocks = own_a.shape[0] - 1
    for j in range(blocks):
        gate_ref[:, j * width : (j + 1) * width] = own_a[j] + a0[j].astype(F32)
        down_ref[j * width : (j + 1) * width, :] = own_b[blocks - 1 + j] + b0[blocks - 1 + j].astype(F32)
    up_ref[:, :width] = own_a[blocks] + a0[blocks].astype(F32)
    for j in range(blocks - 1):
        up_ref[:, (j + 1) * width : (j + 2) * width] = own_b[j] + b0[j].astype(F32)


def back_kernel(width, hidden_ref, gate_pre_ref, up_pre_ref, down_ref, gate_ref, up_ref, _, back_ref, token_ref):
    token_ref[...] = jnp.zeros_like(token_ref)
    model = down_ref.shape[1]
    for j in range(model // width):
        cols = slice(j * width, (j + 1) * width)
        back_ref[:, cols] = dot(hidden_ref[...], down_ref[:, cols]).astype(BF16)
        row_grad = dot(gate_pre_ref[...], gate_ref[cols, :], LAST) + dot(up_pre_ref[...], up_ref[cols, :], LAST)
        back_ref[:, model + j * width : model + (j + 1) * width] = row_grad.astype(BF16)


def combine_kernel(
    capacity, routes_ref, gates_ref, place_ref, grads_ref, back_ref, back_grad_ref,
    out_ref, grad_ref, gates_grad_ref, high, low, score,
):
    step = pl.program_id(0)

    @pl.when(step == 0)
    def _():
        gates_t = gates_ref[...]
        weight = jnp.zeros(place_ref.shape, F32)
        for k, mask in enumerate(slot_masks(routes_ref[...], place_ref.shape[0], capacity)):
            weight = jnp.where(mask, gates_t[k : k + 1, :], weight)
        weight = weight * place_ref[...].astype(F32)
        high[...] = weight.astype(BF16)
        low[...] = (weight - weight.astype(BF16).astype(F32)).astype(BF16)
        score[...] = jnp.zeros_like(score)

    back = back_ref[...]
    out_ref[...] = (dot(high[...], back, FIRST) + dot(low[...], back, FIRST)).astype(BF16)
    grad_ref[...] = dot(place_ref[...], back_grad_ref[...], FIRST).astype(BF16)
    slot_grads = dot(place_ref[...], grads_ref[...])
    score[...] += jnp.sum(slot_grads * back.astype(F32), axis=1, keepdims=True)

    @pl.when(step == pl.num_programs(0) - 1)
    def _():
        placed = score[...] * place_ref[...].astype(F32)
        for k, mask in enumerate(slot_masks(routes_ref[...], place_ref.shape[0], capacity)):
            gates_grad_ref[k : k + 1, :] = jnp.sum(jnp.where(mask, placed, 0.0), axis=0, keepdims=True)


def shape(dims, dtype=BF16):
    return jax.ShapeDtypeStruct(dims, dtype)


def whole(dims):
    return pl.BlockSpec(dims, lambda i: (0,) * len(dims))


def local(tokens, routes, gate_weights, w_gate, w_up, w_down, out_grad):
    count, top = routes.shape
    model = tokens.shape[1]
    experts = w_gate.shape[0] * lax.axis_size("expert")
    groups = lax.axis_size("dp")
    capacity = max(2, 4 * count * top // (3 * experts))
    slots = experts * capacity
    hid = w_gate.shape[2]
    width = model // groups
    blocks = hid // width
    w_gate, w_up, w_down = w_gate[0], w_up[0], w_down[0]
    routes_t, gates_t = routes.T, gate_weights.T

    resident = pl.BlockSpec(memory_space=pltpu.VMEM)
    anywhere = pl.BlockSpec(memory_space=pl.ANY)
    half = model // 2
    send, place = pl.pallas_call(
        functools.partial(dispatch_kernel, capacity),
        grid=(4,),
        in_specs=[
            whole((top, count)),
            whole((top, count)),
            pl.BlockSpec((count, half), lambda i: (0, jnp.minimum(i, 1))),
            pl.BlockSpec((count, half), lambda i: (0, jnp.maximum(i - 2, 0))),
        ],
        out_specs=[pl.BlockSpec((slots, half), lambda i: (0, i)), whole((slots, count))],
        out_shape=(shape((slots, 2 * model)), shape((slots, count))),
        scratch_shapes=[pltpu.VMEM((slots, 1), F32)],
        compiler_params=params(58),
        cost_estimate=cost(4 * slots * count * model, 4 * slots * model),
        name="dispatch",
    )(routes_t, gates_t, tokens, out_grad)

    def exchange(array):
        wide = array.reshape(experts, capacity, array.shape[1])
        return lax.all_to_all(wide, "expert", 0, 0, tiled=True).reshape(array.shape)

    wide = exchange(send)
    tile = pl.BlockSpec((slots, width), lambda i: (0, i))
    hidden, hidden_t, gate_pre, up_pre = pl.pallas_call(
        expert_kernel,
        grid=(blocks,),
        in_specs=[
            pl.BlockSpec((slots, model), lambda i: (0, 0)),
            pl.BlockSpec((slots, model), lambda i: (0, 1)),
            pl.BlockSpec((model, width), lambda i: (0, i)),
            pl.BlockSpec((model, width), lambda i: (0, i)),
            pl.BlockSpec((width, model), lambda i: (i, 0)),
        ],
        out_specs=[tile, pl.BlockSpec((width, slots), lambda i: (i, 0)), tile, tile],
        out_shape=(shape((slots, hid)), shape((hid, slots)), shape((slots, hid)), shape((slots, hid))),
        compiler_params=params(54),
        cost_estimate=cost(6 * slots * model * hid, 4 * slots * model + 6 * model * hid + 8 * slots * hid),
        name="expert",
    )(wide, wide, w_gate, w_up, w_down)

    me = lax.axis_index("dp")
    place_of = me.reshape(1).astype(jnp.int32)

    def chain_call(step_a, step_b, dtype, held, name, after):
        parts = (shape((blocks + 1, width, width), dtype), shape((2 * blocks - 1, width, width), dtype))
        return pl.pallas_call(
            functools.partial(link_kernel, bool(held)),
            grid_spec=pltpu.PrefetchScalarGridSpec(
                num_scalar_prefetch=1,
                grid=(1,),
                in_specs=[
                    pl.BlockSpec((slots, width), lambda i, p: (0, lax.rem(p[0] + step_a, groups))),
                    pl.BlockSpec((slots, width), lambda i, p: (0, lax.rem(p[0] + step_b, groups))),
                    pl.BlockSpec((slots, width), lambda i, p: (0, groups + lax.rem(p[0] + step_b, groups))),
                    *[resident] * (3 + len(held)),
                    *[anywhere] * len(after),
                ],
                out_specs=[resident, resident],
            ),
            out_shape=parts,
            compiler_params=params(),
            cost_estimate=LONG,
            name=name,
        )(place_of, wide, wide, wide, gate_pre, up_pre, hidden_t, *held, *after)

    up_ring = [(i, (i + 1) % groups) for i in range(groups)]
    down_ring = [(i, (i - 1) % groups) for i in range(groups)]
    half_way = groups // 2
    slots_of_ring = [(half_way, 0)] + [(k, s) for k in range(half_way - 1, 0, -1) for s in (1, 0)]
    def rows_back(after):
        return pl.pallas_call(
            functools.partial(back_kernel, width),
            in_specs=[*[resident] * 6, anywhere],
            out_specs=[resident] * 2,
            out_shape=(shape((slots, 2 * model)), shape((8, 128), F32)),
            compiler_params=params(),
            cost_estimate=SHORT,
            name="rows_back",
        )(hidden, gate_pre, up_pre, w_down, w_gate, w_up, after)

    came, after = {}, ()
    for number, (k, swapped) in enumerate(slots_of_ring):
        step_a, step_b = (groups - k, k) if swapped else (k, groups - k)
        held = came.get((k, swapped), ())
        part_a, part_b = chain_call(step_a, step_b, BF16, held, f"chain_sum_{number}", after)
        after = (part_a,)
        if number == 1:
            going_back, token = rows_back(part_a)
            after = (token,)
        ring_a, ring_b = (down_ring, up_ring) if swapped else (up_ring, down_ring)
        came[k - 1, swapped] = (lax.ppermute(part_a, "dp", ring_a), lax.ppermute(part_b, "dp", ring_b))

    back = exchange(going_back)

    layer_out, token_grad, gates_grad_t = pl.pallas_call(
        functools.partial(combine_kernel, capacity),
        grid=(2,),
        in_specs=[
            whole((top, count)),
            whole((top, count)),
            whole((slots, count)),
            pl.BlockSpec((count, half), lambda i: (0, i)),
            pl.BlockSpec((slots, half), lambda i: (0, i)),
            pl.BlockSpec((slots, half), lambda i: (0, 2 + i)),
        ],
        out_specs=[
            pl.BlockSpec((count, half), lambda i: (0, i)),
            pl.BlockSpec((count, half), lambda i: (0, i)),
            whole((top, count)),
        ],
        out_shape=(shape((count, model)), shape((count, model)), shape((top, count), F32)),
        scratch_shapes=[pltpu.VMEM((slots, count), BF16)] * 2 + [pltpu.VMEM((slots, 1), F32)],
        compiler_params=params(),
        cost_estimate=cost(8 * slots * count * model, 4 * slots * model),
        name="combine",
    )(routes_t, gates_t, place, out_grad, back, back)

    own_a, own_b = chain_call(0, 0, F32, came[0, 1], "chain_sum_own", (*after, token_grad))
    gate_grad, up_grad, down_grad = pl.pallas_call(
        last_kernel,
        in_specs=[resident] * 4,
        out_shape=(shape((width, hid), F32), shape((width, hid), F32), shape((hid, width), F32)),
        compiler_params=params(),
        cost_estimate=SHORT,
        name="chain_sum_last",
    )(own_a, own_b, *came[0, 0])
    return (layer_out, token_grad, gates_grad_t.T, gate_grad[None], up_grad[None], down_grad[None])


def solution(mesh):
    rows = P(("expert", "dp"), None)
    weights = P("expert", None, None)
    return jax.shard_map(
        local,
        mesh=mesh,
        in_specs=(rows, rows, rows, weights, weights, weights, rows),
        out_specs=(rows, rows, rows, P("expert", "dp", None), P("expert", "dp", None), P("expert", None, "dp")),
        check_vma=False,
    )
```

```python
import functools

import jax
import jax.numpy as jnp
from jax import lax
from jax.experimental import pallas as pl
from jax.experimental.pallas import tpu as pltpu
from jax.sharding import PartitionSpec as P

BF16 = jnp.bfloat16
F32 = jnp.float32
LAST = (((1,), (1,)), ((), ()))
FIRST = (((0,), (0,)), ((), ()))


def params(mib=16):
    return pltpu.CompilerParams(vmem_limit_bytes=mib * 2**20)


def cost(flops, nbytes, exps=0):
    return pl.CostEstimate(flops=flops, bytes_accessed=nbytes, transcendentals=exps)


LONG = cost(20 * 10**9, 60 * 2**20)
SHORT = cost(1, 1)


def dot(a, b, dims=(((1,), (0,)), ((), ()))):
    return lax.dot_general(a, b, dims, preferred_element_type=F32)


def slot_masks(routes_t, slots, capacity):
    tokens = routes_t.shape[1]
    expert = lax.broadcasted_iota(jnp.int32, (slots, tokens), 0) // capacity
    return [expert == routes_t[k : k + 1, :] for k in range(routes_t.shape[0])]


def dispatch_kernel(capacity, routes_ref, gates_ref, tokens_ref, grads_ref, wide_ref, place_ref, slot_weight):
    step, half = pl.program_id(0), pl.num_programs(0) // 2

    @pl.when(step == 0)
    def _():
        slots, tokens = place_ref.shape
        hit = jnp.zeros((slots, tokens), F32)
        weight = jnp.zeros((slots, tokens), F32)
        gates_t = gates_ref[...]
        for k, mask in enumerate(slot_masks(routes_ref[...], slots, capacity)):
            hit = jnp.where(mask, 1.0, hit)
            weight = jnp.where(mask, gates_t[k : k + 1, :], weight)
        before = (
            lax.broadcasted_iota(jnp.int32, (tokens, tokens), 0)
            < lax.broadcasted_iota(jnp.int32, (tokens, tokens), 1)
        ).astype(F32).astype(BF16)
        rank = dot(hit.astype(BF16), before)
        mine = (lax.broadcasted_iota(jnp.int32, (slots, tokens), 0) % capacity).astype(F32)
        place = jnp.where(rank == mine, hit, 0.0)
        slot_weight[...] = jnp.sum(place * weight, axis=1, keepdims=True)
        place_ref[...] = place.astype(BF16)

    @pl.when(step < half)
    def _():
        wide_ref[...] = dot(place_ref[...], tokens_ref[...]).astype(BF16)

    @pl.when(step >= half)
    def _():
        wide_ref[...] = (slot_weight[...] * dot(place_ref[...], grads_ref[...])).astype(BF16)


def expert_kernel(rows_ref, grads_ref, gate_ref, up_ref, down_ref, hidden_ref, hidden_t_ref, gate_pre_ref, up_pre_ref):
    width = gate_ref.shape[1]
    mine = pl.ds(pl.multiple_of(pl.program_id(0) * width, width), width)
    rows = rows_ref[...]
    pre_gate = dot(rows, gate_ref[...])
    pre_up = dot(rows, up_ref[...])
    hidden_grad = dot(grads_ref[...], down_ref[...], LAST)
    sig = jax.nn.sigmoid(pre_gate)
    silu = pre_gate * sig
    hidden = (silu * pre_up).astype(BF16)
    hidden_ref[:, mine] = hidden
    hidden_t_ref[mine, :] = hidden.T
    gate_pre_ref[:, mine] = (hidden_grad * pre_up * sig * (1.0 + pre_gate * (1.0 - sig))).astype(BF16)
    up_pre_ref[:, mine] = (hidden_grad * silu).astype(BF16)


def chunk_sums(rows_a, rows_b, grads_b, gate_pre, up_pre, hidden_t, held_a=(), held_b=()):
    width = rows_a.shape[1]
    blocks = gate_pre.shape[1] // width
    turned_a, turned_b, grads = rows_a[...].T, rows_b[...].T, grads_b[...]
    for j in range(blocks + 1):
        source = gate_pre[:, j * width : (j + 1) * width] if j < blocks else up_pre[:, :width]
        total = dot(turned_a, source)
        for held in held_a:
            total = total + held[j].astype(F32)
        yield "a", j, total
    for j in range(2 * blocks - 1):
        if j < blocks - 1:
            total = dot(turned_b, up_pre[:, (j + 1) * width : (j + 2) * width])
        else:
            i = j - blocks + 1
            total = dot(hidden_t[i * width : (i + 1) * width, :], grads)
        for held in held_b:
            total = total + held[j].astype(F32)
        yield "b", j, total


def link_kernel(arrived, _, *refs):
    held = [[refs[6]], [refs[7]]] if arrived else []
    out = {"a": refs[-2], "b": refs[-1]}
    for part, j, total in chunk_sums(*refs[:6], *held):
        out[part][j] = total.astype(out[part].dtype)


def last_kernel(own_a, own_b, a0, b0, gate_ref, up_ref, down_ref):
    width = own_a.shape[1]
    blocks = own_a.shape[0] - 1
    for j in range(blocks):
        gate_ref[:, j * width : (j + 1) * width] = own_a[j] + a0[j].astype(F32)
        down_ref[j * width : (j + 1) * width, :] = own_b[blocks - 1 + j] + b0[blocks - 1 + j].astype(F32)
    up_ref[:, :width] = own_a[blocks] + a0[blocks].astype(F32)
    for j in range(blocks - 1):
        up_ref[:, (j + 1) * width : (j + 2) * width] = own_b[j] + b0[j].astype(F32)


def back_kernel(width, hidden_ref, gate_pre_ref, up_pre_ref, down_ref, gate_ref, up_ref, _, back_ref, token_ref):
    token_ref[...] = jnp.zeros_like(token_ref)
    model = down_ref.shape[1]
    for j in range(model // width):
        cols = slice(j * width, (j + 1) * width)
        back_ref[:, cols] = dot(hidden_ref[...], down_ref[:, cols]).astype(BF16)
        row_grad = dot(gate_pre_ref[...], gate_ref[cols, :], LAST) + dot(up_pre_ref[...], up_ref[cols, :], LAST)
        back_ref[:, model + j * width : model + (j + 1) * width] = row_grad.astype(BF16)


def combine_kernel(
    capacity, routes_ref, gates_ref, place_ref, grads_ref, back_ref, back_grad_ref,
    out_ref, grad_ref, gates_grad_ref, high, low, score,
):
    step = pl.program_id(0)

    @pl.when(step == 0)
    def _():
        gates_t = gates_ref[...]
        weight = jnp.zeros(place_ref.shape, F32)
        for k, mask in enumerate(slot_masks(routes_ref[...], place_ref.shape[0], capacity)):
            weight = jnp.where(mask, gates_t[k : k + 1, :], weight)
        weight = weight * place_ref[...].astype(F32)
        high[...] = weight.astype(BF16)
        low[...] = (weight - weight.astype(BF16).astype(F32)).astype(BF16)
        score[...] = jnp.zeros_like(score)

    back = back_ref[...]
    out_ref[...] = (dot(high[...], back, FIRST) + dot(low[...], back, FIRST)).astype(BF16)
    grad_ref[...] = dot(place_ref[...], back_grad_ref[...], FIRST).astype(BF16)
    slot_grads = dot(place_ref[...], grads_ref[...])
    score[...] += jnp.sum(slot_grads * back.astype(F32), axis=1, keepdims=True)

    @pl.when(step == pl.num_programs(0) - 1)
    def _():
        placed = score[...] * place_ref[...].astype(F32)
        for k, mask in enumerate(slot_masks(routes_ref[...], place_ref.shape[0], capacity)):
            gates_grad_ref[k : k + 1, :] = jnp.sum(jnp.where(mask, placed, 0.0), axis=0, keepdims=True)


def shape(dims, dtype=BF16):
    return jax.ShapeDtypeStruct(dims, dtype)


def whole(dims):
    return pl.BlockSpec(dims, lambda i: (0,) * len(dims))


def local(tokens, routes, gate_weights, w_gate, w_up, w_down, out_grad):
    count, top = routes.shape
    model = tokens.shape[1]
    experts = w_gate.shape[0] * lax.axis_size("expert")
    groups = lax.axis_size("dp")
    capacity = max(2, 4 * count * top // (3 * experts))
    slots = experts * capacity
    hid = w_gate.shape[2]
    width = model // groups
    blocks = hid // width
    w_gate, w_up, w_down = w_gate[0], w_up[0], w_down[0]
    routes_t, gates_t = routes.T, gate_weights.T

    resident = pl.BlockSpec(memory_space=pltpu.VMEM)
    anywhere = pl.BlockSpec(memory_space=pl.ANY)
    half = model // 2
    send, place = pl.pallas_call(
        functools.partial(dispatch_kernel, capacity),
        grid=(4,),
        in_specs=[
            whole((top, count)),
            whole((top, count)),
            pl.BlockSpec((count, half), lambda i: (0, jnp.minimum(i, 1))),
            pl.BlockSpec((count, half), lambda i: (0, jnp.maximum(i - 2, 0))),
        ],
        out_specs=[pl.BlockSpec((slots, half), lambda i: (0, i)), whole((slots, count))],
        out_shape=(shape((slots, 2 * model)), shape((slots, count))),
        scratch_shapes=[pltpu.VMEM((slots, 1), F32)],
        compiler_params=params(58),
        cost_estimate=cost(4 * slots * count * model, 4 * slots * model),
        name="dispatch",
    )(routes_t, gates_t, tokens, out_grad)

    def exchange(array):
        wide = array.reshape(experts, capacity, array.shape[1])
        return lax.all_to_all(wide, "expert", 0, 0, tiled=True).reshape(array.shape)

    wide = exchange(send)
    hidden, hidden_t, gate_pre, up_pre = pl.pallas_call(
        expert_kernel,
        grid=(blocks,),
        in_specs=[
            pl.BlockSpec((slots, model), lambda i: (0, 0)),
            pl.BlockSpec((slots, model), lambda i: (0, 1)),
            pl.BlockSpec((model, width), lambda i: (0, i)),
            pl.BlockSpec((model, width), lambda i: (0, i)),
            pl.BlockSpec((width, model), lambda i: (i, 0)),
        ],
        out_specs=[resident] * 4,
        out_shape=(shape((slots, hid)), shape((hid, slots)), shape((slots, hid)), shape((slots, hid))),
        compiler_params=params(50),
        cost_estimate=cost(6 * slots * model * hid, 4 * slots * model + 6 * model * hid + 8 * slots * hid),
        name="expert",
    )(wide, wide, w_gate, w_up, w_down)

    me = lax.axis_index("dp")
    place_of = me.reshape(1).astype(jnp.int32)

    def chain_call(step_a, step_b, dtype, held, name, after):
        parts = (shape((blocks + 1, width, width), dtype), shape((2 * blocks - 1, width, width), dtype))
        return pl.pallas_call(
            functools.partial(link_kernel, bool(held)),
            grid_spec=pltpu.PrefetchScalarGridSpec(
                num_scalar_prefetch=1,
                grid=(1,),
                in_specs=[
                    pl.BlockSpec((slots, width), lambda i, p: (0, lax.rem(p[0] + step_a, groups))),
                    pl.BlockSpec((slots, width), lambda i, p: (0, lax.rem(p[0] + step_b, groups))),
                    pl.BlockSpec((slots, width), lambda i, p: (0, groups + lax.rem(p[0] + step_b, groups))),
                    *[resident] * (3 + len(held)),
                    *[anywhere] * len(after),
                ],
                out_specs=[resident, resident],
            ),
            out_shape=parts,
            compiler_params=params(),
            cost_estimate=LONG,
            name=name,
        )(place_of, wide, wide, wide, gate_pre, up_pre, hidden_t, *held, *after)

    up_ring = [(i, (i + 1) % groups) for i in range(groups)]
    down_ring = [(i, (i - 1) % groups) for i in range(groups)]
    half_way = groups // 2
    slots_of_ring = [(half_way, 0)] + [(k, s) for k in range(half_way - 1, 0, -1) for s in (1, 0)]
    def rows_back(after):
        return pl.pallas_call(
            functools.partial(back_kernel, width),
            in_specs=[*[resident] * 6, anywhere],
            out_specs=[resident] * 2,
            out_shape=(shape((slots, 2 * model)), shape((8, 128), F32)),
            compiler_params=params(),
            cost_estimate=SHORT,
            name="rows_back",
        )(hidden, gate_pre, up_pre, w_down, w_gate, w_up, after)

    came, after = {}, ()
    for number, (k, swapped) in enumerate(slots_of_ring):
        step_a, step_b = (groups - k, k) if swapped else (k, groups - k)
        held = came.get((k, swapped), ())
        part_a, part_b = chain_call(step_a, step_b, BF16, held, f"chain_sum_{number}", after)
        after = (part_a,)
        if number == 2:
            going_back, token = rows_back(part_a)
            after = (token,)
        ring_a, ring_b = (down_ring, up_ring) if swapped else (up_ring, down_ring)
        came[k - 1, swapped] = (lax.ppermute(part_a, "dp", ring_a), lax.ppermute(part_b, "dp", ring_b))

    back = exchange(going_back)

    layer_out, token_grad, gates_grad_t = pl.pallas_call(
        functools.partial(combine_kernel, capacity),
        grid=(2,),
        in_specs=[
            whole((top, count)),
            whole((top, count)),
            whole((slots, count)),
            pl.BlockSpec((count, half), lambda i: (0, i)),
            pl.BlockSpec((slots, half), lambda i: (0, i)),
            pl.BlockSpec((slots, half), lambda i: (0, 2 + i)),
        ],
        out_specs=[
            pl.BlockSpec((count, half), lambda i: (0, i)),
            pl.BlockSpec((count, half), lambda i: (0, i)),
            whole((top, count)),
        ],
        out_shape=(shape((count, model)), shape((count, model)), shape((top, count), F32)),
        scratch_shapes=[pltpu.VMEM((slots, count), BF16)] * 2 + [pltpu.VMEM((slots, 1), F32)],
        compiler_params=params(),
        cost_estimate=cost(8 * slots * count * model, 4 * slots * model),
        name="combine",
    )(routes_t, gates_t, place, out_grad, back, back)

    own_a, own_b = chain_call(0, 0, F32, came[0, 1], "chain_sum_own", (*after, token_grad))
    gate_grad, up_grad, down_grad = pl.pallas_call(
        last_kernel,
        in_specs=[resident] * 4,
        out_shape=(shape((width, hid), F32), shape((width, hid), F32), shape((hid, width), F32)),
        compiler_params=params(),
        cost_estimate=SHORT,
        name="chain_sum_last",
    )(own_a, own_b, *came[0, 0])
    return (layer_out, token_grad, gates_grad_t.T, gate_grad[None], up_grad[None], down_grad[None])


def solution(mesh):
    rows = P(("expert", "dp"), None)
    weights = P("expert", None, None)
    return jax.shard_map(
        local,
        mesh=mesh,
        in_specs=(rows, rows, rows, weights, weights, weights, rows),
        out_specs=(rows, rows, rows, P("expert", "dp", None), P("expert", "dp", None), P("expert", None, "dp")),
        check_vma=False,
    )
```

```python
import functools

import jax
import jax.numpy as jnp
from jax import lax
from jax.experimental import pallas as pl
from jax.experimental.pallas import tpu as pltpu
from jax.sharding import PartitionSpec as P

BF16 = jnp.bfloat16
F32 = jnp.float32
LAST = (((1,), (1,)), ((), ()))
FIRST = (((0,), (0,)), ((), ()))


def params(mib=16):
    return pltpu.CompilerParams(vmem_limit_bytes=mib * 2**20)


def cost(flops, nbytes, exps=0):
    return pl.CostEstimate(flops=flops, bytes_accessed=nbytes, transcendentals=exps)


LONG = cost(20 * 10**9, 60 * 2**20)
SHORT = cost(1, 1)


def dot(a, b, dims=(((1,), (0,)), ((), ()))):
    return lax.dot_general(a, b, dims, preferred_element_type=F32)


def slot_masks(routes_t, slots, capacity):
    tokens = routes_t.shape[1]
    expert = lax.broadcasted_iota(jnp.int32, (slots, tokens), 0) // capacity
    return [expert == routes_t[k : k + 1, :] for k in range(routes_t.shape[0])]


def dispatch_kernel(capacity, routes_ref, gates_ref, tokens_ref, grads_ref, wide_ref, place_ref, slot_weight):
    step = pl.program_id(0)

    @pl.when(step == 0)
    def _():
        slots, tokens = place_ref.shape
        hit = jnp.zeros((slots, tokens), F32)
        weight = jnp.zeros((slots, tokens), F32)
        gates_t = gates_ref[...]
        for k, mask in enumerate(slot_masks(routes_ref[...], slots, capacity)):
            hit = jnp.where(mask, 1.0, hit)
            weight = jnp.where(mask, gates_t[k : k + 1, :], weight)
        before = (
            lax.broadcasted_iota(jnp.int32, (tokens, tokens), 0)
            < lax.broadcasted_iota(jnp.int32, (tokens, tokens), 1)
        ).astype(F32).astype(BF16)
        rank = dot(hit.astype(BF16), before)
        mine = (lax.broadcasted_iota(jnp.int32, (slots, tokens), 0) % capacity).astype(F32)
        place = jnp.where(rank == mine, hit, 0.0)
        slot_weight[...] = jnp.sum(place * weight, axis=1, keepdims=True)
        place_ref[...] = place.astype(BF16)

    @pl.when(step == 0)
    def _():
        wide_ref[...] = dot(place_ref[...], tokens_ref[...]).astype(BF16)

    @pl.when(step == 1)
    def _():
        wide_ref[...] = (slot_weight[...] * dot(place_ref[...], grads_ref[...])).astype(BF16)


def expert_kernel(rows_ref, grads_ref, gate_ref, up_ref, down_ref, hidden_ref, hidden_t_ref, gate_pre_ref, up_pre_ref):
    width = gate_ref.shape[1]
    mine = pl.ds(pl.multiple_of(pl.program_id(0) * width, width), width)
    rows = rows_ref[...]
    pre_gate = dot(rows, gate_ref[...])
    pre_up = dot(rows, up_ref[...])
    hidden_grad = dot(grads_ref[...], down_ref[...], LAST)
    sig = jax.nn.sigmoid(pre_gate)
    silu = pre_gate * sig
    hidden = (silu * pre_up).astype(BF16)
    hidden_ref[:, mine] = hidden
    hidden_t_ref[mine, :] = hidden.T
    gate_pre_ref[:, mine] = (hidden_grad * pre_up * sig * (1.0 + pre_gate * (1.0 - sig))).astype(BF16)
    up_pre_ref[:, mine] = (hidden_grad * silu).astype(BF16)


def chunk_sums(rows_a, rows_b, grads_b, gate_pre, up_pre, hidden_t, held_a=(), held_b=()):
    width = rows_a.shape[1]
    blocks = gate_pre.shape[1] // width
    turned_a, turned_b, grads = rows_a[...].T, rows_b[...].T, grads_b[...]
    for j in range(blocks + 1):
        source = gate_pre[:, j * width : (j + 1) * width] if j < blocks else up_pre[:, :width]
        total = dot(turned_a, source)
        for held in held_a:
            total = total + held[j].astype(F32)
        yield "a", j, total
    for j in range(2 * blocks - 1):
        if j < blocks - 1:
            total = dot(turned_b, up_pre[:, (j + 1) * width : (j + 2) * width])
        else:
            i = j - blocks + 1
            total = dot(hidden_t[i * width : (i + 1) * width, :], grads)
        for held in held_b:
            total = total + held[j].astype(F32)
        yield "b", j, total


def link_kernel(arrived, _, *refs):
    held = [[refs[6]], [refs[7]]] if arrived else []
    out = {"a": refs[-2], "b": refs[-1]}
    for part, j, total in chunk_sums(*refs[:6], *held):
        out[part][j] = total.astype(out[part].dtype)


def last_kernel(own_a, own_b, a0, b0, _, gate_ref, up_ref, down_ref):
    width = own_a.shape[1]
    blocks = own_a.shape[0] - 1
    for j in range(blocks):
        gate_ref[:, j * width : (j + 1) * width] = own_a[j] + a0[j].astype(F32)
        down_ref[j * width : (j + 1) * width, :] = own_b[blocks - 1 + j] + b0[blocks - 1 + j].astype(F32)
    up_ref[:, :width] = own_a[blocks] + a0[blocks].astype(F32)
    for j in range(blocks - 1):
        up_ref[:, (j + 1) * width : (j + 2) * width] = own_b[j] + b0[j].astype(F32)


def back_kernel(hidden_ref, gate_pre_ref, up_pre_ref, down_ref, gate_ref, up_ref, _, back_ref, token_ref):
    width = gate_ref.shape[0]
    token_ref[...] = jnp.zeros_like(token_ref)
    back_ref[:, :width] = dot(hidden_ref[...], down_ref[...]).astype(BF16)
    row_grad = dot(gate_pre_ref[...], gate_ref[...], LAST) + dot(up_pre_ref[...], up_ref[...], LAST)
    back_ref[:, width:] = row_grad.astype(BF16)


def combine_kernel(
    capacity, width, routes_ref, gates_ref, place_ref, grads_ref, back_ref,
    out_ref, grad_ref, gates_grad_ref, high, low, place_t, score,
):
    step = pl.program_id(0)

    @pl.when(step == 0)
    def _():
        gates_t = gates_ref[...]
        place = place_ref[...].astype(F32)
        weight = jnp.zeros(place.shape, F32)
        for k, mask in enumerate(slot_masks(routes_ref[...], place.shape[0], capacity)):
            weight = jnp.where(mask, gates_t[k : k + 1, :], weight)
        weight = (weight * place).T
        high[...] = weight.astype(BF16)
        low[...] = (weight - weight.astype(BF16).astype(F32)).astype(BF16)
        place_t[...] = place.T.astype(BF16)
        score[...] = jnp.zeros_like(score)

    for j in range(grads_ref.shape[1] // width):
        cols = slice(j * width, (j + 1) * width)
        back = back_ref[:, 2 * j * width : (2 * j + 1) * width]
        out_ref[:, cols] = (dot(high[...], back) + dot(low[...], back)).astype(BF16)
        grad_ref[:, cols] = dot(place_t[...], back_ref[:, (2 * j + 1) * width : (2 * j + 2) * width]).astype(BF16)
        slot_grads = dot(place_ref[...], grads_ref[:, cols])
        score[...] += jnp.sum(slot_grads * back.astype(F32), axis=1, keepdims=True)

    @pl.when(step == pl.num_programs(0) - 1)
    def _():
        placed = score[...] * place_ref[...].astype(F32)
        for k, mask in enumerate(slot_masks(routes_ref[...], place_ref.shape[0], capacity)):
            gates_grad_ref[k : k + 1, :] = jnp.sum(jnp.where(mask, placed, 0.0), axis=0, keepdims=True)


def shape(dims, dtype=BF16):
    return jax.ShapeDtypeStruct(dims, dtype)


def whole(dims):
    return pl.BlockSpec(dims, lambda i: (0,) * len(dims))


def local(tokens, routes, gate_weights, w_gate, w_up, w_down, out_grad):
    count, top = routes.shape
    model = tokens.shape[1]
    experts = w_gate.shape[0] * lax.axis_size("expert")
    groups = lax.axis_size("dp")
    capacity = max(2, 4 * count * top // (3 * experts))
    slots = experts * capacity
    hid = w_gate.shape[2]
    width = model // groups
    blocks = hid // width
    w_gate, w_up, w_down = w_gate[0], w_up[0], w_down[0]
    routes_t, gates_t = routes.T, gate_weights.T

    resident = pl.BlockSpec(memory_space=pltpu.VMEM)
    anywhere = pl.BlockSpec(memory_space=pl.ANY)
    half = model // 2
    send, place = pl.pallas_call(
        functools.partial(dispatch_kernel, capacity),
        grid=(2,),
        in_specs=[
            whole((top, count)),
            whole((top, count)),
            whole((count, model)),
            whole((count, model)),
        ],
        out_specs=[pl.BlockSpec((slots, model), lambda i: (0, i)), whole((slots, count))],
        out_shape=(shape((slots, 2 * model)), shape((slots, count))),
        scratch_shapes=[pltpu.VMEM((slots, 1), F32)],
        compiler_params=params(58),
        cost_estimate=cost(4 * slots * count * model, 4 * slots * model),
        name="dispatch",
    )(routes_t, gates_t, tokens, out_grad)

    def exchange(array):
        wide = array.reshape(experts, capacity, array.shape[1])
        return lax.all_to_all(wide, "expert", 0, 0, tiled=True).reshape(array.shape)

    wide = exchange(send)
    hidden, hidden_t, gate_pre, up_pre = pl.pallas_call(
        expert_kernel,
        grid=(blocks,),
        in_specs=[
            pl.BlockSpec((slots, model), lambda i: (0, 0)),
            pl.BlockSpec((slots, model), lambda i: (0, 1)),
            pl.BlockSpec((model, width), lambda i: (0, i)),
            pl.BlockSpec((model, width), lambda i: (0, i)),
            pl.BlockSpec((width, model), lambda i: (i, 0)),
        ],
        out_specs=[resident] * 4,
        out_shape=(shape((slots, hid)), shape((hid, slots)), shape((slots, hid)), shape((slots, hid))),
        compiler_params=params(50),
        cost_estimate=cost(6 * slots * model * hid, 4 * slots * model + 6 * model * hid + 8 * slots * hid),
        name="expert",
    )(wide, wide, w_gate, w_up, w_down)

    me = lax.axis_index("dp")
    place_of = me.reshape(1).astype(jnp.int32)

    def chain_call(step_a, step_b, dtype, held, name, after):
        parts = (shape((blocks + 1, width, width), dtype), shape((2 * blocks - 1, width, width), dtype))
        return pl.pallas_call(
            functools.partial(link_kernel, bool(held)),
            grid_spec=pltpu.PrefetchScalarGridSpec(
                num_scalar_prefetch=1,
                grid=(1,),
                in_specs=[
                    pl.BlockSpec((slots, width), lambda i, p: (0, lax.rem(p[0] + step_a, groups))),
                    pl.BlockSpec((slots, width), lambda i, p: (0, lax.rem(p[0] + step_b, groups))),
                    pl.BlockSpec((slots, width), lambda i, p: (0, groups + lax.rem(p[0] + step_b, groups))),
                    *[resident] * (3 + len(held)),
                    *[anywhere] * len(after),
                ],
                out_specs=[resident, resident],
            ),
            out_shape=parts,
            compiler_params=params(),
            cost_estimate=LONG,
            name=name,
        )(place_of, wide, wide, wide, gate_pre, up_pre, hidden_t, *held, *after)

    up_ring = [(i, (i + 1) % groups) for i in range(groups)]
    down_ring = [(i, (i - 1) % groups) for i in range(groups)]
    half_way = groups // 2
    slots_of_ring = [(half_way, 0)] + [(k, s) for k in range(half_way - 1, 0, -1) for s in (1, 0)]
    def rows_back(after):
        return pl.pallas_call(
            back_kernel,
            grid=(groups,),
            in_specs=[
                *[resident] * 3,
                pl.BlockSpec((hid, width), lambda i: (0, i)),
                pl.BlockSpec((width, hid), lambda i: (i, 0)),
                pl.BlockSpec((width, hid), lambda i: (i, 0)),
                anywhere,
            ],
            out_specs=[pl.BlockSpec((slots, 2 * width), lambda i: (0, i)), whole((8, 128))],
            out_shape=(shape((slots, 2 * model)), shape((8, 128), F32)),
            compiler_params=params(50),
            cost_estimate=SHORT,
            name="rows_back",
        )(hidden, gate_pre, up_pre, w_down, w_gate, w_up, after)

    came, after = {}, ()
    for number, (k, swapped) in enumerate(slots_of_ring):
        step_a, step_b = (groups - k, k) if swapped else (k, groups - k)
        held = came.get((k, swapped), ())
        part_a, part_b = chain_call(step_a, step_b, BF16, held, f"chain_sum_{number}", after)
        after = (part_a,)
        if number == 1:
            going_back, token = rows_back(part_a)
            after = (token,)
        ring_a, ring_b = (down_ring, up_ring) if swapped else (up_ring, down_ring)
        came[k - 1, swapped] = (lax.ppermute(part_a, "dp", ring_a), lax.ppermute(part_b, "dp", ring_b))

    back = exchange(going_back)

    layer_out, token_grad, gates_grad_t = pl.pallas_call(
        functools.partial(combine_kernel, capacity, width),
        grid=(2,),
        in_specs=[
            whole((top, count)),
            whole((top, count)),
            whole((slots, count)),
            pl.BlockSpec((count, half), lambda i: (0, i)),
            pl.BlockSpec((slots, model), lambda i: (0, i)),
        ],
        out_specs=[
            pl.BlockSpec((count, half), lambda i: (0, i)),
            pl.BlockSpec((count, half), lambda i: (0, i)),
            whole((top, count)),
        ],
        out_shape=(shape((count, model)), shape((count, model)), shape((top, count), F32)),
        scratch_shapes=[pltpu.VMEM((count, slots), BF16)] * 3 + [pltpu.VMEM((slots, 1), F32)],
        compiler_params=params(40),
        cost_estimate=cost(8 * slots * count * model, 4 * slots * model),
        name="combine",
    )(routes_t, gates_t, place, out_grad, back)

    own_a, own_b = chain_call(0, 0, F32, came[0, 1], "chain_sum_own", after)
    gate_grad, up_grad, down_grad = pl.pallas_call(
        last_kernel,
        in_specs=[*[resident] * 4, anywhere],
        out_shape=(shape((width, hid), F32), shape((width, hid), F32), shape((hid, width), F32)),
        compiler_params=params(),
        cost_estimate=SHORT,
        name="chain_sum_last",
    )(own_a, own_b, *came[0, 0], gates_grad_t)
    return (layer_out, token_grad, gates_grad_t.T, gate_grad[None], up_grad[None], down_grad[None])


def solution(mesh):
    rows = P(("expert", "dp"), None)
    weights = P("expert", None, None)
    return jax.shard_map(
        local,
        mesh=mesh,
        in_specs=(rows, rows, rows, weights, weights, weights, rows),
        out_specs=(rows, rows, rows, P("expert", "dp", None), P("expert", "dp", None), P("expert", None, "dp")),
        check_vma=False,
    )
```

```python
import functools

import jax
import jax.numpy as jnp
from jax import lax
from jax.experimental import pallas as pl
from jax.experimental.pallas import tpu as pltpu
from jax.sharding import PartitionSpec as P

BF16 = jnp.bfloat16
F32 = jnp.float32
LAST = (((1,), (1,)), ((), ()))
FIRST = (((0,), (0,)), ((), ()))


def params(mib=16):
    return pltpu.CompilerParams(vmem_limit_bytes=mib * 2**20)


def cost(flops, nbytes, exps=0):
    return pl.CostEstimate(flops=flops, bytes_accessed=nbytes, transcendentals=exps)


LONG = cost(20 * 10**9, 60 * 2**20)
SHORT = cost(1, 1)


def dot(a, b, dims=(((1,), (0,)), ((), ()))):
    return lax.dot_general(a, b, dims, preferred_element_type=F32)


def slot_masks(routes_t, slots, capacity):
    tokens = routes_t.shape[1]
    expert = lax.broadcasted_iota(jnp.int32, (slots, tokens), 0) // capacity
    return [expert == routes_t[k : k + 1, :] for k in range(routes_t.shape[0])]


def dispatch_kernel(capacity, routes_ref, gates_ref, tokens_ref, grads_ref, wide_ref, place_ref, slot_weight):
    step = pl.program_id(0)

    @pl.when(step == 0)
    def _():
        slots, tokens = place_ref.shape
        hit = jnp.zeros((slots, tokens), F32)
        weight = jnp.zeros((slots, tokens), F32)
        gates_t = gates_ref[...]
        for k, mask in enumerate(slot_masks(routes_ref[...], slots, capacity)):
            hit = jnp.where(mask, 1.0, hit)
            weight = jnp.where(mask, gates_t[k : k + 1, :], weight)
        before = (
            lax.broadcasted_iota(jnp.int32, (tokens, tokens), 0)
            < lax.broadcasted_iota(jnp.int32, (tokens, tokens), 1)
        ).astype(F32).astype(BF16)
        rank = dot(hit.astype(BF16), before)
        mine = (lax.broadcasted_iota(jnp.int32, (slots, tokens), 0) % capacity).astype(F32)
        place = jnp.where(rank == mine, hit, 0.0)
        slot_weight[...] = jnp.sum(place * weight, axis=1, keepdims=True)
        place_ref[...] = place.astype(BF16)

    @pl.when(step == 0)
    def _():
        wide_ref[...] = dot(place_ref[...], tokens_ref[...]).astype(BF16)

    @pl.when(step == 1)
    def _():
        wide_ref[...] = (slot_weight[...] * dot(place_ref[...], grads_ref[...])).astype(BF16)


def expert_kernel(rows_ref, grads_ref, gate_ref, up_ref, down_ref, hidden_ref, hidden_t_ref, gate_pre_ref, up_pre_ref):
    width = gate_ref.shape[1]
    mine = pl.ds(pl.multiple_of(pl.program_id(0) * width, width), width)
    rows = rows_ref[...]
    pre_gate = dot(rows, gate_ref[...])
    pre_up = dot(rows, up_ref[...])
    hidden_grad = dot(grads_ref[...], down_ref[...], LAST)
    sig = jax.nn.sigmoid(pre_gate)
    silu = pre_gate * sig
    hidden = (silu * pre_up).astype(BF16)
    hidden_ref[:, mine] = hidden
    hidden_t_ref[mine, :] = hidden.T
    gate_pre_ref[:, mine] = (hidden_grad * pre_up * sig * (1.0 + pre_gate * (1.0 - sig))).astype(BF16)
    up_pre_ref[:, mine] = (hidden_grad * silu).astype(BF16)


def chunk_sums(rows_a, rows_b, grads_b, gate_pre, up_pre, hidden_t, held_a=(), held_b=()):
    width = rows_a.shape[1]
    blocks = gate_pre.shape[1] // width
    turned_a, turned_b, grads = rows_a[...].T, rows_b[...].T, grads_b[...]
    for j in range(blocks + 1):
        source = gate_pre[:, j * width : (j + 1) * width] if j < blocks else up_pre[:, :width]
        total = dot(turned_a, source)
        for held in held_a:
            total = total + held[j].astype(F32)
        yield "a", j, total
    for j in range(2 * blocks - 1):
        if j < blocks - 1:
            total = dot(turned_b, up_pre[:, (j + 1) * width : (j + 2) * width])
        else:
            i = j - blocks + 1
            total = dot(hidden_t[i * width : (i + 1) * width, :], grads)
        for held in held_b:
            total = total + held[j].astype(F32)
        yield "b", j, total


def link_kernel(arrived, _, *refs):
    held = [[refs[6]], [refs[7]]] if arrived else []
    out = {"a": refs[-2], "b": refs[-1]}
    for part, j, total in chunk_sums(*refs[:6], *held):
        out[part][j] = total.astype(out[part].dtype)


def last_kernel(own_a, own_b, a0, b0, _, gate_ref, up_ref, down_ref):
    width = own_a.shape[1]
    blocks = own_a.shape[0] - 1
    for j in range(blocks):
        gate_ref[:, j * width : (j + 1) * width] = own_a[j] + a0[j].astype(F32)
        down_ref[j * width : (j + 1) * width, :] = own_b[blocks - 1 + j] + b0[blocks - 1 + j].astype(F32)
    up_ref[:, :width] = own_a[blocks] + a0[blocks].astype(F32)
    for j in range(blocks - 1):
        up_ref[:, (j + 1) * width : (j + 2) * width] = own_b[j] + b0[j].astype(F32)


def back_kernel(width, hidden_ref, gate_pre_ref, up_pre_ref, down_ref, gate_ref, up_ref, _, back_ref, token_ref):
    token_ref[...] = jnp.zeros_like(token_ref)
    for j in range(back_ref.shape[1] // (2 * width)):
        first = pl.program_id(0) * (back_ref.shape[1] // 2) + j * width
        mine = pl.ds(pl.multiple_of(first, width), width)
        at = 2 * j * width
        back_ref[:, at : at + width] = dot(hidden_ref[...], down_ref[:, mine]).astype(BF16)
        row_grad = dot(gate_pre_ref[...], gate_ref[mine, :], LAST) + dot(up_pre_ref[...], up_ref[mine, :], LAST)
        back_ref[:, at + width : at + 2 * width] = row_grad.astype(BF16)


def combine_kernel(
    capacity, width, routes_ref, gates_ref, place_ref, grads_ref, back_ref,
    out_ref, grad_ref, gates_grad_ref, high, low, place_t, score,
):
    step = pl.program_id(0)

    @pl.when(step == 0)
    def _():
        gates_t = gates_ref[...]
        place = place_ref[...].astype(F32)
        weight = jnp.zeros(place.shape, F32)
        for k, mask in enumerate(slot_masks(routes_ref[...], place.shape[0], capacity)):
            weight = jnp.where(mask, gates_t[k : k + 1, :], weight)
        weight = (weight * place).T
        high[...] = weight.astype(BF16)
        low[...] = (weight - weight.astype(BF16).astype(F32)).astype(BF16)
        place_t[...] = place.T.astype(BF16)
        score[...] = jnp.zeros_like(score)

    for j in range(grads_ref.shape[1] // width):
        cols = slice(j * width, (j + 1) * width)
        back = back_ref[:, 2 * j * width : (2 * j + 1) * width]
        out_ref[:, cols] = (dot(high[...], back) + dot(low[...], back)).astype(BF16)
        grad_ref[:, cols] = dot(place_t[...], back_ref[:, (2 * j + 1) * width : (2 * j + 2) * width]).astype(BF16)
        slot_grads = dot(place_ref[...], grads_ref[:, cols])
        score[...] += jnp.sum(slot_grads * back.astype(F32), axis=1, keepdims=True)

    @pl.when(step == pl.num_programs(0) - 1)
    def _():
        placed = score[...] * place_ref[...].astype(F32)
        for k, mask in enumerate(slot_masks(routes_ref[...], place_ref.shape[0], capacity)):
            gates_grad_ref[k : k + 1, :] = jnp.sum(jnp.where(mask, placed, 0.0), axis=0, keepdims=True)


def shape(dims, dtype=BF16):
    return jax.ShapeDtypeStruct(dims, dtype)


def whole(dims):
    return pl.BlockSpec(dims, lambda i: (0,) * len(dims))


def local(tokens, routes, gate_weights, w_gate, w_up, w_down, out_grad):
    count, top = routes.shape
    model = tokens.shape[1]
    experts = w_gate.shape[0] * lax.axis_size("expert")
    groups = lax.axis_size("dp")
    capacity = max(2, 4 * count * top // (3 * experts))
    slots = experts * capacity
    hid = w_gate.shape[2]
    width = model // groups
    blocks = hid // width
    w_gate, w_up, w_down = w_gate[0], w_up[0], w_down[0]
    routes_t, gates_t = routes.T, gate_weights.T

    resident = pl.BlockSpec(memory_space=pltpu.VMEM)
    anywhere = pl.BlockSpec(memory_space=pl.ANY)
    half = model // 2
    send, place = pl.pallas_call(
        functools.partial(dispatch_kernel, capacity),
        grid=(2,),
        in_specs=[
            whole((top, count)),
            whole((top, count)),
            whole((count, model)),
            whole((count, model)),
        ],
        out_specs=[pl.BlockSpec((slots, model), lambda i: (0, i)), whole((slots, count))],
        out_shape=(shape((slots, 2 * model)), shape((slots, count))),
        scratch_shapes=[pltpu.VMEM((slots, 1), F32)],
        compiler_params=params(58),
        cost_estimate=cost(4 * slots * count * model, 4 * slots * model),
        name="dispatch",
    )(routes_t, gates_t, tokens, out_grad)

    def exchange(array):
        wide = array.reshape(experts, capacity, array.shape[1])
        return lax.all_to_all(wide, "expert", 0, 0, tiled=True).reshape(array.shape)

    wide = exchange(send)
    hidden, hidden_t, gate_pre, up_pre = pl.pallas_call(
        expert_kernel,
        grid=(blocks,),
        in_specs=[
            pl.BlockSpec((slots, model), lambda i: (0, 0)),
            pl.BlockSpec((slots, model), lambda i: (0, 1)),
            pl.BlockSpec((model, width), lambda i: (0, i)),
            pl.BlockSpec((model, width), lambda i: (0, i)),
            pl.BlockSpec((width, model), lambda i: (i, 0)),
        ],
        out_specs=[resident] * 4,
        out_shape=(shape((slots, hid)), shape((hid, slots)), shape((slots, hid)), shape((slots, hid))),
        compiler_params=params(50),
        cost_estimate=cost(6 * slots * model * hid, 4 * slots * model + 6 * model * hid + 8 * slots * hid),
        name="expert",
    )(wide, wide, w_gate, w_up, w_down)

    me = lax.axis_index("dp")
    place_of = me.reshape(1).astype(jnp.int32)

    def chain_call(step_a, step_b, dtype, held, name, after):
        parts = (shape((blocks + 1, width, width), dtype), shape((2 * blocks - 1, width, width), dtype))
        return pl.pallas_call(
            functools.partial(link_kernel, bool(held)),
            grid_spec=pltpu.PrefetchScalarGridSpec(
                num_scalar_prefetch=1,
                grid=(1,),
                in_specs=[
                    pl.BlockSpec((slots, width), lambda i, p: (0, lax.rem(p[0] + step_a, groups))),
                    pl.BlockSpec((slots, width), lambda i, p: (0, lax.rem(p[0] + step_b, groups))),
                    pl.BlockSpec((slots, width), lambda i, p: (0, groups + lax.rem(p[0] + step_b, groups))),
                    *[resident] * (3 + len(held)),
                    *[anywhere] * len(after),
                ],
                out_specs=[resident, resident],
            ),
            out_shape=parts,
            compiler_params=params(),
            cost_estimate=LONG,
            name=name,
        )(place_of, wide, wide, wide, gate_pre, up_pre, hidden_t, *held, *after)

    up_ring = [(i, (i + 1) % groups) for i in range(groups)]
    down_ring = [(i, (i - 1) % groups) for i in range(groups)]
    half_way = groups // 2
    slots_of_ring = [(half_way, 0)] + [(k, s) for k in range(half_way - 1, 0, -1) for s in (1, 0)]
    def rows_back(after):
        return pl.pallas_call(
            functools.partial(back_kernel, width),
            grid=(groups // 2,),
            in_specs=[*[resident] * 6, anywhere],
            out_specs=[pl.BlockSpec((slots, 4 * width), lambda i: (0, i)), whole((8, 128))],
            out_shape=(shape((slots, 2 * model)), shape((8, 128), F32)),
            compiler_params=params(40),
            cost_estimate=SHORT,
            name="rows_back",
        )(hidden, gate_pre, up_pre, w_down, w_gate, w_up, after)

    came, after = {}, ()
    for number, (k, swapped) in enumerate(slots_of_ring):
        step_a, step_b = (groups - k, k) if swapped else (k, groups - k)
        held = came.get((k, swapped), ())
        part_a, part_b = chain_call(step_a, step_b, BF16, held, f"chain_sum_{number}", after)
        after = (part_a,)
        if number == 1:
            going_back, token = rows_back(part_a)
            after = (token,)
        ring_a, ring_b = (down_ring, up_ring) if swapped else (up_ring, down_ring)
        came[k - 1, swapped] = (lax.ppermute(part_a, "dp", ring_a), lax.ppermute(part_b, "dp", ring_b))

    back = exchange(going_back)

    layer_out, token_grad, gates_grad_t = pl.pallas_call(
        functools.partial(combine_kernel, capacity, width),
        grid=(2,),
        in_specs=[
            whole((top, count)),
            whole((top, count)),
            whole((slots, count)),
            pl.BlockSpec((count, half), lambda i: (0, i)),
            pl.BlockSpec((slots, model), lambda i: (0, i)),
        ],
        out_specs=[
            pl.BlockSpec((count, half), lambda i: (0, i)),
            pl.BlockSpec((count, half), lambda i: (0, i)),
            whole((top, count)),
        ],
        out_shape=(shape((count, model)), shape((count, model)), shape((top, count), F32)),
        scratch_shapes=[pltpu.VMEM((count, slots), BF16)] * 3 + [pltpu.VMEM((slots, 1), F32)],
        compiler_params=params(40),
        cost_estimate=cost(8 * slots * count * model, 4 * slots * model),
        name="combine",
    )(routes_t, gates_t, place, out_grad, back)

    own_a, own_b = chain_call(0, 0, F32, came[0, 1], "chain_sum_own", after)
    gate_grad, up_grad, down_grad = pl.pallas_call(
        last_kernel,
        in_specs=[*[resident] * 4, anywhere],
        out_shape=(shape((width, hid), F32), shape((width, hid), F32), shape((hid, width), F32)),
        compiler_params=params(),
        cost_estimate=SHORT,
        name="chain_sum_last",
    )(own_a, own_b, *came[0, 0], gates_grad_t)
    return (layer_out, token_grad, gates_grad_t.T, gate_grad[None], up_grad[None], down_grad[None])


def solution(mesh):
    rows = P(("expert", "dp"), None)
    weights = P("expert", None, None)
    return jax.shard_map(
        local,
        mesh=mesh,
        in_specs=(rows, rows, rows, weights, weights, weights, rows),
        out_specs=(rows, rows, rows, P("expert", "dp", None), P("expert", "dp", None), P("expert", None, "dp")),
        check_vma=False,
    )
```

```python
import functools

import jax
import jax.numpy as jnp
from jax import lax
from jax.experimental import pallas as pl
from jax.experimental.pallas import tpu as pltpu
from jax.sharding import PartitionSpec as P

BF16 = jnp.bfloat16
F32 = jnp.float32
LAST = (((1,), (1,)), ((), ()))
FIRST = (((0,), (0,)), ((), ()))


def params(mib=16):
    return pltpu.CompilerParams(vmem_limit_bytes=mib * 2**20)


def cost(flops, nbytes, exps=0):
    return pl.CostEstimate(flops=flops, bytes_accessed=nbytes, transcendentals=exps)


LONG = cost(20 * 10**9, 60 * 2**20)
SHORT = cost(1, 1)


def dot(a, b, dims=(((1,), (0,)), ((), ()))):
    return lax.dot_general(a, b, dims, preferred_element_type=F32)


def slot_masks(routes_t, slots, capacity):
    tokens = routes_t.shape[1]
    expert = lax.broadcasted_iota(jnp.int32, (slots, tokens), 0) // capacity
    return [expert == routes_t[k : k + 1, :] for k in range(routes_t.shape[0])]


def dispatch_kernel(capacity, routes_ref, gates_ref, tokens_ref, grads_ref, wide_ref, place_ref, slot_weight):
    step = pl.program_id(0)

    @pl.when(step == 0)
    def _():
        slots, tokens = place_ref.shape
        hit = jnp.zeros((slots, tokens), F32)
        weight = jnp.zeros((slots, tokens), F32)
        gates_t = gates_ref[...]
        for k, mask in enumerate(slot_masks(routes_ref[...], slots, capacity)):
            hit = jnp.where(mask, 1.0, hit)
            weight = jnp.where(mask, gates_t[k : k + 1, :], weight)
        before = (
            lax.broadcasted_iota(jnp.int32, (tokens, tokens), 0)
            < lax.broadcasted_iota(jnp.int32, (tokens, tokens), 1)
        ).astype(F32).astype(BF16)
        rank = dot(hit.astype(BF16), before)
        mine = (lax.broadcasted_iota(jnp.int32, (slots, tokens), 0) % capacity).astype(F32)
        place = jnp.where(rank == mine, hit, 0.0)
        slot_weight[...] = jnp.sum(place * weight, axis=1, keepdims=True)
        place_ref[...] = place.astype(BF16)

    @pl.when(step == 0)
    def _():
        wide_ref[...] = dot(place_ref[...], tokens_ref[...]).astype(BF16)

    @pl.when(step == 1)
    def _():
        wide_ref[...] = (slot_weight[...] * dot(place_ref[...], grads_ref[...])).astype(BF16)


def expert_kernel(rows_ref, grads_ref, gate_ref, up_ref, down_ref, hidden_ref, hidden_t_ref, gate_pre_ref, up_pre_ref):
    width = gate_ref.shape[1]
    mine = pl.ds(pl.multiple_of(pl.program_id(0) * width, width), width)
    rows = rows_ref[...]
    pre_gate = dot(rows, gate_ref[...])
    pre_up = dot(rows, up_ref[...])
    hidden_grad = dot(grads_ref[...], down_ref[...], LAST)
    sig = jax.nn.sigmoid(pre_gate)
    silu = pre_gate * sig
    hidden = (silu * pre_up).astype(BF16)
    hidden_ref[:, mine] = hidden
    hidden_t_ref[mine, :] = hidden.T
    gate_pre_ref[:, mine] = (hidden_grad * pre_up * sig * (1.0 + pre_gate * (1.0 - sig))).astype(BF16)
    up_pre_ref[:, mine] = (hidden_grad * silu).astype(BF16)


def chunk_sums(rows_a, rows_b, grads_b, gate_pre, up_pre, hidden_t, held_a=(), held_b=()):
    width = rows_a.shape[1]
    blocks = gate_pre.shape[1] // width
    turned_a, turned_b, grads = rows_a[...].T, rows_b[...].T, grads_b[...]
    for j in range(blocks + 1):
        source = gate_pre[:, j * width : (j + 1) * width] if j < blocks else up_pre[:, :width]
        total = dot(turned_a, source)
        for held in held_a:
            total = total + held[j].astype(F32)
        yield "a", j, total
    for j in range(2 * blocks - 1):
        if j < blocks - 1:
            total = dot(turned_b, up_pre[:, (j + 1) * width : (j + 2) * width])
        else:
            i = j - blocks + 1
            total = dot(hidden_t[i * width : (i + 1) * width, :], grads)
        for held in held_b:
            total = total + held[j].astype(F32)
        yield "b", j, total


def link_kernel(arrived, _, *refs):
    held = [[refs[6]], [refs[7]]] if arrived else []
    out = {"a": refs[-2], "b": refs[-1]}
    for part, j, total in chunk_sums(*refs[:6], *held):
        out[part][j] = total.astype(out[part].dtype)


def last_kernel(own_a, own_b, a0, b0, gate_ref, up_ref, down_ref):
    width = own_a.shape[1]
    blocks = own_a.shape[0] - 1
    for j in range(blocks):
        gate_ref[:, j * width : (j + 1) * width] = own_a[j] + a0[j].astype(F32)
        down_ref[j * width : (j + 1) * width, :] = own_b[blocks - 1 + j] + b0[blocks - 1 + j].astype(F32)
    up_ref[:, :width] = own_a[blocks] + a0[blocks].astype(F32)
    for j in range(blocks - 1):
        up_ref[:, (j + 1) * width : (j + 2) * width] = own_b[j] + b0[j].astype(F32)


def back_kernel(width, hidden_ref, gate_pre_ref, up_pre_ref, down_ref, gate_ref, up_ref, _, back_ref, token_ref):
    token_ref[...] = jnp.zeros_like(token_ref)
    for j in range(back_ref.shape[1] // (2 * width)):
        first = pl.program_id(0) * (back_ref.shape[1] // 2) + j * width
        mine = pl.ds(pl.multiple_of(first, width), width)
        at = 2 * j * width
        back_ref[:, at : at + width] = dot(hidden_ref[...], down_ref[:, mine]).astype(BF16)
        row_grad = dot(gate_pre_ref[...], gate_ref[mine, :], LAST) + dot(up_pre_ref[...], up_ref[mine, :], LAST)
        back_ref[:, at + width : at + 2 * width] = row_grad.astype(BF16)


def combine_kernel(
    capacity, width, routes_ref, gates_ref, place_ref, grads_ref, back_ref,
    out_ref, grad_ref, gates_grad_ref, token_ref, high, low, place_t, score,
):
    step = pl.program_id(0)
    token_ref[...] = jnp.zeros_like(token_ref)

    @pl.when(step == 0)
    def _():
        gates_t = gates_ref[...]
        place = place_ref[...].astype(F32)
        weight = jnp.zeros(place.shape, F32)
        for k, mask in enumerate(slot_masks(routes_ref[...], place.shape[0], capacity)):
            weight = jnp.where(mask, gates_t[k : k + 1, :], weight)
        weight = (weight * place).T
        high[...] = weight.astype(BF16)
        low[...] = (weight - weight.astype(BF16).astype(F32)).astype(BF16)
        place_t[...] = place.T.astype(BF16)
        score[...] = jnp.zeros_like(score)

    for j in range(grads_ref.shape[1] // width):
        cols = slice(j * width, (j + 1) * width)
        back = back_ref[:, 2 * j * width : (2 * j + 1) * width]
        out_ref[:, cols] = (dot(high[...], back) + dot(low[...], back)).astype(BF16)
        grad_ref[:, cols] = dot(place_t[...], back_ref[:, (2 * j + 1) * width : (2 * j + 2) * width]).astype(BF16)
        slot_grads = dot(place_ref[...], grads_ref[:, cols])
        score[...] += jnp.sum(slot_grads * back.astype(F32), axis=1, keepdims=True)

    @pl.when(step == pl.num_programs(0) - 1)
    def _():
        placed = score[...] * place_ref[...].astype(F32)
        for k, mask in enumerate(slot_masks(routes_ref[...], place_ref.shape[0], capacity)):
            gates_grad_ref[k : k + 1, :] = jnp.sum(jnp.where(mask, placed, 0.0), axis=0, keepdims=True)


def shape(dims, dtype=BF16):
    return jax.ShapeDtypeStruct(dims, dtype)


def whole(dims):
    return pl.BlockSpec(dims, lambda i: (0,) * len(dims))


def local(tokens, routes, gate_weights, w_gate, w_up, w_down, out_grad):
    count, top = routes.shape
    model = tokens.shape[1]
    experts = w_gate.shape[0] * lax.axis_size("expert")
    groups = lax.axis_size("dp")
    capacity = max(2, 4 * count * top // (3 * experts))
    slots = experts * capacity
    hid = w_gate.shape[2]
    width = model // groups
    blocks = hid // width
    w_gate, w_up, w_down = w_gate[0], w_up[0], w_down[0]
    routes_t, gates_t = routes.T, gate_weights.T

    resident = pl.BlockSpec(memory_space=pltpu.VMEM)
    anywhere = pl.BlockSpec(memory_space=pl.ANY)
    half = model // 2
    send, place = pl.pallas_call(
        functools.partial(dispatch_kernel, capacity),
        grid=(2,),
        in_specs=[
            whole((top, count)),
            whole((top, count)),
            whole((count, model)),
            whole((count, model)),
        ],
        out_specs=[pl.BlockSpec((slots, model), lambda i: (0, i)), whole((slots, count))],
        out_shape=(shape((slots, 2 * model)), shape((slots, count))),
        scratch_shapes=[pltpu.VMEM((slots, 1), F32)],
        compiler_params=params(58),
        cost_estimate=cost(4 * slots * count * model, 4 * slots * model),
        name="dispatch",
    )(routes_t, gates_t, tokens, out_grad)

    def exchange(array):
        wide = array.reshape(experts, capacity, array.shape[1])
        return lax.all_to_all(wide, "expert", 0, 0, tiled=True).reshape(array.shape)

    wide = exchange(send)
    hidden, hidden_t, gate_pre, up_pre = pl.pallas_call(
        expert_kernel,
        grid=(blocks,),
        in_specs=[
            pl.BlockSpec((slots, model), lambda i: (0, 0)),
            pl.BlockSpec((slots, model), lambda i: (0, 1)),
            pl.BlockSpec((model, width), lambda i: (0, i)),
            pl.BlockSpec((model, width), lambda i: (0, i)),
            pl.BlockSpec((width, model), lambda i: (i, 0)),
        ],
        out_specs=[resident] * 4,
        out_shape=(shape((slots, hid)), shape((hid, slots)), shape((slots, hid)), shape((slots, hid))),
        compiler_params=params(50),
        cost_estimate=cost(6 * slots * model * hid, 4 * slots * model + 6 * model * hid + 8 * slots * hid),
        name="expert",
    )(wide, wide, w_gate, w_up, w_down)

    me = lax.axis_index("dp")
    place_of = me.reshape(1).astype(jnp.int32)

    def chain_call(step_a, step_b, dtype, held, name, after):
        parts = (shape((blocks + 1, width, width), dtype), shape((2 * blocks - 1, width, width), dtype))
        return pl.pallas_call(
            functools.partial(link_kernel, bool(held)),
            grid_spec=pltpu.PrefetchScalarGridSpec(
                num_scalar_prefetch=1,
                grid=(1,),
                in_specs=[
                    pl.BlockSpec((slots, width), lambda i, p: (0, lax.rem(p[0] + step_a, groups))),
                    pl.BlockSpec((slots, width), lambda i, p: (0, lax.rem(p[0] + step_b, groups))),
                    pl.BlockSpec((slots, width), lambda i, p: (0, groups + lax.rem(p[0] + step_b, groups))),
                    *[resident] * (3 + len(held)),
                    *[anywhere] * len(after),
                ],
                out_specs=[resident, resident],
            ),
            out_shape=parts,
            compiler_params=params(),
            cost_estimate=LONG,
            name=name,
        )(place_of, wide, wide, wide, gate_pre, up_pre, hidden_t, *held, *after)

    up_ring = [(i, (i + 1) % groups) for i in range(groups)]
    down_ring = [(i, (i - 1) % groups) for i in range(groups)]
    half_way = groups // 2
    slots_of_ring = [(half_way, 0)] + [(k, s) for k in range(half_way - 1, 0, -1) for s in (1, 0)]
    def rows_back(after):
        return pl.pallas_call(
            functools.partial(back_kernel, width),
            grid=(groups // 2,),
            in_specs=[*[resident] * 6, anywhere],
            out_specs=[pl.BlockSpec((slots, 4 * width), lambda i: (0, i)), whole((8, 128))],
            out_shape=(shape((slots, 2 * model)), shape((8, 128), F32)),
            compiler_params=params(40),
            cost_estimate=SHORT,
            name="rows_back",
        )(hidden, gate_pre, up_pre, w_down, w_gate, w_up, after)

    came, after = {}, ()
    for number, (k, swapped) in enumerate(slots_of_ring):
        step_a, step_b = (groups - k, k) if swapped else (k, groups - k)
        held = came.get((k, swapped), ())
        part_a, part_b = chain_call(step_a, step_b, BF16, held, f"chain_sum_{number}", after)
        after = (part_a,)
        if number == 1:
            going_back, token = rows_back(part_a)
            after = (token,)
        ring_a, ring_b = (down_ring, up_ring) if swapped else (up_ring, down_ring)
        came[k - 1, swapped] = (lax.ppermute(part_a, "dp", ring_a), lax.ppermute(part_b, "dp", ring_b))

    back = exchange(going_back)

    layer_out, token_grad, gates_grad_t, token = pl.pallas_call(
        functools.partial(combine_kernel, capacity, width),
        grid=(2,),
        in_specs=[
            whole((top, count)),
            whole((top, count)),
            whole((slots, count)),
            pl.BlockSpec((count, half), lambda i: (0, i)),
            pl.BlockSpec((slots, model), lambda i: (0, i)),
        ],
        out_specs=[
            pl.BlockSpec((count, half), lambda i: (0, i)),
            pl.BlockSpec((count, half), lambda i: (0, i)),
            whole((top, count)),
            whole((8, 128)),
        ],
        out_shape=(shape((count, model)), shape((count, model)), shape((top, count), F32), shape((8, 128), F32)),
        scratch_shapes=[pltpu.VMEM((count, slots), BF16)] * 3 + [pltpu.VMEM((slots, 1), F32)],
        compiler_params=params(40),
        cost_estimate=cost(8 * slots * count * model, 4 * slots * model),
        name="combine",
    )(routes_t, gates_t, place, out_grad, back)

    own_a, own_b = chain_call(0, 0, F32, came[0, 1], "chain_sum_own", (*after, token))
    gate_grad, up_grad, down_grad = pl.pallas_call(
        last_kernel,
        in_specs=[resident] * 4,
        out_shape=(shape((width, hid), F32), shape((width, hid), F32), shape((hid, width), F32)),
        compiler_params=params(),
        cost_estimate=SHORT,
        name="chain_sum_last",
    )(own_a, own_b, *came[0, 0])
    return (layer_out, token_grad, gates_grad_t.T, gate_grad[None], up_grad[None], down_grad[None])


def solution(mesh):
    rows = P(("expert", "dp"), None)
    weights = P("expert", None, None)
    return jax.shard_map(
        local,
        mesh=mesh,
        in_specs=(rows, rows, rows, weights, weights, weights, rows),
        out_specs=(rows, rows, rows, P("expert", "dp", None), P("expert", "dp", None), P("expert", None, "dp")),
        check_vma=False,
    )
```

```python
import functools

import jax
import jax.numpy as jnp
from jax import lax
from jax.experimental import pallas as pl
from jax.experimental.pallas import tpu as pltpu
from jax.sharding import PartitionSpec as P

BF16 = jnp.bfloat16
F32 = jnp.float32
LAST = (((1,), (1,)), ((), ()))
FIRST = (((0,), (0,)), ((), ()))


def params(mib=16):
    return pltpu.CompilerParams(vmem_limit_bytes=mib * 2**20)


def cost(flops, nbytes, exps=0):
    return pl.CostEstimate(flops=flops, bytes_accessed=nbytes, transcendentals=exps)


LONG = cost(20 * 10**9, 60 * 2**20)
SHORT = cost(1, 1)


def dot(a, b, dims=(((1,), (0,)), ((), ()))):
    return lax.dot_general(a, b, dims, preferred_element_type=F32)


def slot_masks(routes_t, slots, capacity):
    tokens = routes_t.shape[1]
    expert = lax.broadcasted_iota(jnp.int32, (slots, tokens), 0) // capacity
    return [expert == routes_t[k : k + 1, :] for k in range(routes_t.shape[0])]


def dispatch_kernel(capacity, routes_ref, gates_ref, tokens_ref, grads_ref, wide_ref, place_ref):
    slots, tokens = place_ref.shape
    model = tokens_ref.shape[1]
    hit = jnp.zeros((slots, tokens), F32)
    weight = jnp.zeros((slots, tokens), F32)
    gates_t = gates_ref[...]
    for k, mask in enumerate(slot_masks(routes_ref[...], slots, capacity)):
        hit = jnp.where(mask, 1.0, hit)
        weight = jnp.where(mask, gates_t[k : k + 1, :], weight)
    before = (
        lax.broadcasted_iota(jnp.int32, (tokens, tokens), 0) < lax.broadcasted_iota(jnp.int32, (tokens, tokens), 1)
    ).astype(F32).astype(BF16)
    rank = dot(hit.astype(BF16), before)
    mine = (lax.broadcasted_iota(jnp.int32, (slots, tokens), 0) % capacity).astype(F32)
    place = jnp.where(rank == mine, hit, 0.0)
    slot_weight = jnp.sum(place * weight, axis=1, keepdims=True)
    place_low = place.astype(BF16)
    place_ref[...] = place_low
    wide_ref[:, :model] = dot(place_low, tokens_ref[...]).astype(BF16)
    wide_ref[:, model:] = (slot_weight * dot(place_low, grads_ref[...])).astype(BF16)


def expert_kernel(rows_ref, grads_ref, gate_ref, up_ref, down_ref, hidden_ref, hidden_t_ref, gate_pre_ref, up_pre_ref):
    width = gate_ref.shape[1]
    mine = pl.ds(pl.multiple_of(pl.program_id(0) * width, width), width)
    rows = rows_ref[...]
    pre_gate = dot(rows, gate_ref[...])
    pre_up = dot(rows, up_ref[...])
    hidden_grad = dot(grads_ref[...], down_ref[...], LAST)
    sig = jax.nn.sigmoid(pre_gate)
    silu = pre_gate * sig
    hidden = (silu * pre_up).astype(BF16)
    hidden_ref[:, mine] = hidden
    hidden_t_ref[mine, :] = hidden.T
    gate_pre_ref[:, mine] = (hidden_grad * pre_up * sig * (1.0 + pre_gate * (1.0 - sig))).astype(BF16)
    up_pre_ref[:, mine] = (hidden_grad * silu).astype(BF16)


def chunk_sums(rows_a, rows_b, grads_b, gate_pre, up_pre, hidden_t, held_a=(), held_b=()):
    width = rows_a.shape[1]
    blocks = gate_pre.shape[1] // width
    turned_a, turned_b, grads = rows_a[...].T, rows_b[...].T, grads_b[...]
    for j in range(blocks + 1):
        source = gate_pre[:, j * width : (j + 1) * width] if j < blocks else up_pre[:, :width]
        total = dot(turned_a, source)
        for held in held_a:
            total = total + held[j].astype(F32)
        yield "a", j, total
    for j in range(2 * blocks - 1):
        if j < blocks - 1:
            total = dot(turned_b, up_pre[:, (j + 1) * width : (j + 2) * width])
        else:
            i = j - blocks + 1
            total = dot(hidden_t[i * width : (i + 1) * width, :], grads)
        for held in held_b:
            total = total + held[j].astype(F32)
        yield "b", j, total


def link_kernel(arrived, _, *refs):
    held = [[refs[6]], [refs[7]]] if arrived else []
    out = {"a": refs[-2], "b": refs[-1]}
    for part, j, total in chunk_sums(*refs[:6], *held):
        out[part][j] = total.astype(out[part].dtype)


def last_kernel(own_a, own_b, a0, b0, gate_ref, up_ref, down_ref):
    width = own_a.shape[1]
    blocks = own_a.shape[0] - 1
    for j in range(blocks):
        gate_ref[:, j * width : (j + 1) * width] = own_a[j] + a0[j].astype(F32)
        down_ref[j * width : (j + 1) * width, :] = own_b[blocks - 1 + j] + b0[blocks - 1 + j].astype(F32)
    up_ref[:, :width] = own_a[blocks] + a0[blocks].astype(F32)
    for j in range(blocks - 1):
        up_ref[:, (j + 1) * width : (j + 2) * width] = own_b[j] + b0[j].astype(F32)


def back_kernel(width, hidden_ref, gate_pre_ref, up_pre_ref, down_ref, gate_ref, up_ref, _, back_ref, token_ref):
    token_ref[...] = jnp.zeros_like(token_ref)
    for j in range(back_ref.shape[1] // (2 * width)):
        first = pl.program_id(0) * (back_ref.shape[1] // 2) + j * width
        mine = pl.ds(pl.multiple_of(first, width), width)
        at = 2 * j * width
        back_ref[:, at : at + width] = dot(hidden_ref[...], down_ref[:, mine]).astype(BF16)
        row_grad = dot(gate_pre_ref[...], gate_ref[mine, :], LAST) + dot(up_pre_ref[...], up_ref[mine, :], LAST)
        back_ref[:, at + width : at + 2 * width] = row_grad.astype(BF16)


def combine_kernel(
    capacity, width, routes_ref, gates_ref, place_ref, grads_ref, back_ref,
    out_ref, grad_ref, gates_grad_ref, token_ref, high, low, place_t, score,
):
    step = pl.program_id(0)
    token_ref[...] = jnp.zeros_like(token_ref)

    @pl.when(step == 0)
    def _():
        gates_t = gates_ref[...]
        place = place_ref[...].astype(F32)
        weight = jnp.zeros(place.shape, F32)
        for k, mask in enumerate(slot_masks(routes_ref[...], place.shape[0], capacity)):
            weight = jnp.where(mask, gates_t[k : k + 1, :], weight)
        weight = (weight * place).T
        high[...] = weight.astype(BF16)
        low[...] = (weight - weight.astype(BF16).astype(F32)).astype(BF16)
        place_t[...] = place.T.astype(BF16)
        score[...] = jnp.zeros_like(score)

    for j in range(grads_ref.shape[1] // width):
        cols = slice(j * width, (j + 1) * width)
        back = back_ref[:, 2 * j * width : (2 * j + 1) * width]
        out_ref[:, cols] = (dot(high[...], back) + dot(low[...], back)).astype(BF16)
        grad_ref[:, cols] = dot(place_t[...], back_ref[:, (2 * j + 1) * width : (2 * j + 2) * width]).astype(BF16)
        slot_grads = dot(place_ref[...], grads_ref[:, cols])
        score[...] += jnp.sum(slot_grads * back.astype(F32), axis=1, keepdims=True)

    @pl.when(step == pl.num_programs(0) - 1)
    def _():
        placed = score[...] * place_ref[...].astype(F32)
        for k, mask in enumerate(slot_masks(routes_ref[...], place_ref.shape[0], capacity)):
            gates_grad_ref[k : k + 1, :] = jnp.sum(jnp.where(mask, placed, 0.0), axis=0, keepdims=True)


def shape(dims, dtype=BF16):
    return jax.ShapeDtypeStruct(dims, dtype)


def whole(dims):
    return pl.BlockSpec(dims, lambda i: (0,) * len(dims))


def local(tokens, routes, gate_weights, w_gate, w_up, w_down, out_grad):
    count, top = routes.shape
    model = tokens.shape[1]
    experts = w_gate.shape[0] * lax.axis_size("expert")
    groups = lax.axis_size("dp")
    capacity = max(2, 4 * count * top // (3 * experts))
    slots = experts * capacity
    hid = w_gate.shape[2]
    width = model // groups
    blocks = hid // width
    w_gate, w_up, w_down = w_gate[0], w_up[0], w_down[0]
    routes_t, gates_t = routes.T, gate_weights.T

    resident = pl.BlockSpec(memory_space=pltpu.VMEM)
    anywhere = pl.BlockSpec(memory_space=pl.ANY)
    half = model // 2
    send, place = pl.pallas_call(
        functools.partial(dispatch_kernel, capacity),
        out_shape=(shape((slots, 2 * model)), shape((slots, count))),
        compiler_params=params(58),
        cost_estimate=cost(4 * slots * count * model, 4 * slots * model),
        name="dispatch",
    )(routes_t, gates_t, tokens, out_grad)

    def exchange(array):
        wide = array.reshape(experts, capacity, array.shape[1])
        return lax.all_to_all(wide, "expert", 0, 0, tiled=True).reshape(array.shape)

    wide = exchange(send)
    hidden, hidden_t, gate_pre, up_pre = pl.pallas_call(
        expert_kernel,
        grid=(blocks,),
        in_specs=[
            pl.BlockSpec((slots, model), lambda i: (0, 0)),
            pl.BlockSpec((slots, model), lambda i: (0, 1)),
            pl.BlockSpec((model, width), lambda i: (0, i)),
            pl.BlockSpec((model, width), lambda i: (0, i)),
            pl.BlockSpec((width, model), lambda i: (i, 0)),
        ],
        out_specs=[resident] * 4,
        out_shape=(shape((slots, hid)), shape((hid, slots)), shape((slots, hid)), shape((slots, hid))),
        compiler_params=params(50),
        cost_estimate=cost(6 * slots * model * hid, 4 * slots * model + 6 * model * hid + 8 * slots * hid),
        name="expert",
    )(wide, wide, w_gate, w_up, w_down)

    me = lax.axis_index("dp")
    place_of = me.reshape(1).astype(jnp.int32)

    def chain_call(step_a, step_b, dtype, held, name, after):
        parts = (shape((blocks + 1, width, width), dtype), shape((2 * blocks - 1, width, width), dtype))
        return pl.pallas_call(
            functools.partial(link_kernel, bool(held)),
            grid_spec=pltpu.PrefetchScalarGridSpec(
                num_scalar_prefetch=1,
                grid=(1,),
                in_specs=[
                    pl.BlockSpec((slots, width), lambda i, p: (0, lax.rem(p[0] + step_a, groups))),
                    pl.BlockSpec((slots, width), lambda i, p: (0, lax.rem(p[0] + step_b, groups))),
                    pl.BlockSpec((slots, width), lambda i, p: (0, groups + lax.rem(p[0] + step_b, groups))),
                    *[resident] * (3 + len(held)),
                    *[anywhere] * len(after),
                ],
                out_specs=[resident, resident],
            ),
            out_shape=parts,
            compiler_params=params(),
            cost_estimate=LONG,
            name=name,
        )(place_of, wide, wide, wide, gate_pre, up_pre, hidden_t, *held, *after)

    up_ring = [(i, (i + 1) % groups) for i in range(groups)]
    down_ring = [(i, (i - 1) % groups) for i in range(groups)]
    half_way = groups // 2
    slots_of_ring = [(half_way, 0)] + [(k, s) for k in range(half_way - 1, 0, -1) for s in (1, 0)]
    def rows_back(after):
        return pl.pallas_call(
            functools.partial(back_kernel, width),
            grid=(groups // 2,),
            in_specs=[*[resident] * 6, anywhere],
            out_specs=[pl.BlockSpec((slots, 4 * width), lambda i: (0, i)), whole((8, 128))],
            out_shape=(shape((slots, 2 * model)), shape((8, 128), F32)),
            compiler_params=params(40),
            cost_estimate=SHORT,
            name="rows_back",
        )(hidden, gate_pre, up_pre, w_down, w_gate, w_up, after)

    came, after = {}, ()
    for number, (k, swapped) in enumerate(slots_of_ring):
        step_a, step_b = (groups - k, k) if swapped else (k, groups - k)
        held = came.get((k, swapped), ())
        part_a, part_b = chain_call(step_a, step_b, BF16, held, f"chain_sum_{number}", after)
        after = (part_a,)
        if number == 1:
            going_back, token = rows_back(part_a)
            after = (token,)
        ring_a, ring_b = (down_ring, up_ring) if swapped else (up_ring, down_ring)
        came[k - 1, swapped] = (lax.ppermute(part_a, "dp", ring_a), lax.ppermute(part_b, "dp", ring_b))

    back = exchange(going_back)

    layer_out, token_grad, gates_grad_t, token = pl.pallas_call(
        functools.partial(combine_kernel, capacity, width),
        grid=(2,),
        in_specs=[
            whole((top, count)),
            whole((top, count)),
            whole((slots, count)),
            pl.BlockSpec((count, half), lambda i: (0, i)),
            pl.BlockSpec((slots, model), lambda i: (0, i)),
        ],
        out_specs=[
            pl.BlockSpec((count, half), lambda i: (0, i)),
            pl.BlockSpec((count, half), lambda i: (0, i)),
            whole((top, count)),
            whole((8, 128)),
        ],
        out_shape=(shape((count, model)), shape((count, model)), shape((top, count), F32), shape((8, 128), F32)),
        scratch_shapes=[pltpu.VMEM((count, slots), BF16)] * 3 + [pltpu.VMEM((slots, 1), F32)],
        compiler_params=params(40),
        cost_estimate=cost(8 * slots * count * model, 4 * slots * model),
        name="combine",
    )(routes_t, gates_t, place, out_grad, back)

    own_a, own_b = chain_call(0, 0, F32, came[0, 1], "chain_sum_own", (*after, token))
    gate_grad, up_grad, down_grad = pl.pallas_call(
        last_kernel,
        in_specs=[resident] * 4,
        out_shape=(shape((width, hid), F32), shape((width, hid), F32), shape((hid, width), F32)),
        compiler_params=params(),
        cost_estimate=SHORT,
        name="chain_sum_last",
    )(own_a, own_b, *came[0, 0])
    return (layer_out, token_grad, gates_grad_t.T, gate_grad[None], up_grad[None], down_grad[None])


def solution(mesh):
    rows = P(("expert", "dp"), None)
    weights = P("expert", None, None)
    return jax.shard_map(
        local,
        mesh=mesh,
        in_specs=(rows, rows, rows, weights, weights, weights, rows),
        out_specs=(rows, rows, rows, P("expert", "dp", None), P("expert", "dp", None), P("expert", None, "dp")),
        check_vma=False,
    )
```
